32 devices in a mesh: dp: 16 (over z, y, core), tensor: 2 (over x).
Axes of the slice: x: 2, y: 2, z: 4, core: 2. Of those that a mesh axis runs over, the one named last changes fastest.
Arguments:
- tokens: bfloat16 [16384, 1024], P(('dp', 'tensor')), may hold values from -6 to 6
- cond: bfloat16 [16, 1024], P('dp'), may hold values from -6 to 6
- cotangent: bfloat16 [16384, 1024], P(('dp', 'tensor')), may hold values from -6 to 6
- w_qkv: bfloat16 [1024, 3, 1024], P('dp', None, 'tensor'), may hold values from -0.1875 to 0.1875
- b_qv: bfloat16 [2, 1024], P(None, ('tensor', 'dp')), may hold values from -2 to 2
- w_proj: bfloat16 [1024, 1024], P('tensor', 'dp'), may hold values from -1 to 1
- b_proj: bfloat16 [1024], P(('tensor', 'dp')), may hold values from -2 to 2
- w_fc1: bfloat16 [1024, 4096], P('dp', 'tensor'), may hold values from -0.1875 to 0.1875
- b_fc1: bfloat16 [4096], P(('tensor', 'dp')), may hold values from -3 to 3
- w_fc2: bfloat16 [4096, 1024], P('tensor', 'dp'), may hold values from -0.09375 to 0.09375
- b_fc2: bfloat16 [1024], P(('tensor', 'dp')), may hold values from -2 to 2
- w_ada: bfloat16 [1024, 6, 1024], P('dp', None, 'tensor'), may hold values from -0.1875 to 0.1875
- b_ada: bfloat16 [6, 1024], P(None, ('tensor', 'dp')), may hold values from -2 to 2
Outputs:
- block_out: bfloat16 [16384, 1024], P(('dp', 'tensor'))
- grad_tokens: bfloat16 [16384, 1024], P(('dp', 'tensor'))
- grad_cond: float32 [16, 1024], P('dp')
- grad_w_qkv: float32 [1024, 3, 1024], P('dp', None, 'tensor')
- grad_b_qv: float32 [2, 1024], P(None, ('tensor', 'dp'))
- grad_w_proj: float32 [1024, 1024], P('tensor', 'dp')
- grad_b_proj: float32 [1024], P(('tensor', 'dp'))
- grad_w_fc1: float32 [1024, 4096], P('dp', 'tensor')
- grad_b_fc1: float32 [4096], P(('tensor', 'dp'))
- grad_w_fc2: float32 [4096, 1024], P('tensor', 'dp')
- grad_b_fc2: float32 [1024], P(('tensor', 'dp'))
- grad_w_ada: float32 [1024, 6, 1024], P('dp', None, 'tensor')
- grad_b_ada: float32 [6, 1024], P(None, ('tensor', 'dp'))
The draws below stay inside these ranges and needn't reach their ends.
All inputs are finite; a program needn't handle non-finite values.
Results may differ from the reference program's by a relative error of at most 0.02.
Values may be sent and summed in bfloat16 or wider, within the bound.
No kernel may reach another device: no remote copies, remote signals or barrier semaphores. Data moves between devices by JAX's collectives and lax.ppermute only.
A program may use at most 256 MiB of HBM per device.

```python
import jax
import jax.numpy as jnp
from jax import lax

D = 1024
HEADS = 16
HEAD_DIM = 64
FF = 4096
LEN = 1024
LATENTS = 16
TOKENS = 16384


def level_of(own_key, dims, shards, low, largest):
    gain, own = 1.0, jax.random.fold_in(own_key, 6)
    for axis_at, parts in shards:
        heights = jnp.exp(jax.random.uniform(jax.random.fold_in(own, axis_at), (parts,), jnp.float32, low / len(shards), largest / len(shards)))
        gain = gain * jnp.repeat(heights, dims[axis_at] // parts).reshape([-1 if axis == axis_at else 1 for axis in range(len(dims))])
    return gain


def bell_draw(stream_key, shape, scale, bound, shards=(), kind=jnp.bfloat16):
    drawn = scale * jax.random.normal(stream_key, shape, jnp.float32)
    if shards:
        drawn = drawn * level_of(stream_key, shape, shards, -0.22, 0.18)
    return jnp.clip(drawn, -bound, bound).astype(kind)


def setup_inputs(seed: int = 0) -> dict:
    streams_of = jax.random.split(jax.random.key(seed), 14)
    return {
        "tokens": bell_draw(streams_of[0], (TOKENS, D), 1.0, 6.0, ((0, 32),)),
        "cond": bell_draw(streams_of[1], (LATENTS, D), 1.0, 6.0, ((0, 16),)),
        "cotangent": bell_draw(streams_of[2], (TOKENS, D), 1.0, 6.0, ((0, 32),)),
        "w_qkv": bell_draw(streams_of[3], (D, 3, D), D ** -0.5, 0.1875, ((0, 16), (2, 2))),
        "b_qv": bell_draw(streams_of[4], (2, D), 0.3, 2.0, ((1, 32),)),
        "w_proj": bell_draw(streams_of[5], (D, D), (D // 32) ** -0.5, 1.0, ((0, 2), (1, 16))),
        "b_proj": bell_draw(streams_of[6], (D,), 0.3, 2.0, ((0, 32),)),
        "w_fc1": bell_draw(streams_of[7], (D, FF), D ** -0.5, 0.1875, ((0, 16), (1, 2))),
        "b_fc1": bell_draw(streams_of[8], (FF,), 0.5, 3.0, ((0, 32),)),
        "w_fc2": bell_draw(streams_of[9], (FF, D), FF ** -0.5, 0.09375, ((0, 2), (1, 16))),
        "b_fc2": bell_draw(streams_of[10], (D,), 0.3, 2.0, ((0, 32),)),
        "w_ada": bell_draw(streams_of[11], (D, 6, D), D ** -0.5, 0.1875, ((0, 16), (2, 2))),
        "b_ada": bell_draw(streams_of[12], (6, D), 0.3, 2.0, ((1, 32),)),
    }


@jax.custom_vjp
def low(v):
    return lax.optimization_barrier(v.astype(jnp.bfloat16)).astype(jnp.float32)

@jax.custom_vjp
def low_back(v):
    return v

def low_keep(v):
    return (low(v), None)

def low_pass(kept, grad):
    return (grad,)

def back_keep(v):
    return (v, None)

def back_low(kept, grad):
    return (low(grad),)
low.defvjp(low_keep, low_pass)
low_back.defvjp(back_keep, back_low)
norm_eps = 1e-06
highest = lax.Precision.HIGHEST

def normalize(values):
    centred = values - lax.optimization_barrier(jnp.mean(values, -1, keepdims=True))
    return centred * lax.rsqrt(lax.optimization_barrier(jnp.mean(centred * centred, -1, keepdims=True)) + norm_eps)

def latent_block(inputs, silu_cond, w_qkv, bias_three, w_proj, b_proj, w_fc1, b_fc1, w_fc2, b_fc2, w_ada, b_ada):
    modul = low_back(jnp.einsum('d,dkc->kc', silu_cond, w_ada, precision=highest) + b_ada)
    hidden_one = low(normalize(inputs) * (1.0 + modul[1]) + modul[0])
    qkv_all = jnp.einsum('rd,dkc->rkc', hidden_one, w_qkv, precision=highest) + bias_three
    qkv_all = low(low_back(qkv_all))
    block_rows = min(512, LEN)
    queries = qkv_all[:, 0].reshape(LEN // block_rows, block_rows, HEADS, HEAD_DIM)
    keys_all = qkv_all[:, 1].reshape(LEN, HEADS, HEAD_DIM)
    values_all = qkv_all[:, 2].reshape(LEN, HEADS, HEAD_DIM)

    def attend(query_block):
        scores = jnp.einsum('qhd,khd->hqk', query_block, keys_all, precision=highest) * HEAD_DIM ** (-0.5)
        scores = low_back(scores)
        probs = jax.nn.softmax(scores, axis=-1)
        return jnp.einsum('hqk,khd->qhd', low(probs), values_all, precision=highest)
    attended = lax.map(jax.checkpoint(attend), queries).reshape(LEN, D)
    attended = low(low_back(attended))
    branch_attn = low_back(jnp.dot(attended, w_proj, precision=highest) + b_proj)
    middle = inputs + modul[2] * branch_attn
    hidden_two = low(normalize(middle) * (1.0 + modul[4]) + modul[3])
    pre_act = low_back(jnp.dot(hidden_two, w_fc1, precision=highest) + b_fc1)
    activ = low(jax.nn.gelu(pre_act, approximate=True))
    branch_mlp = low_back(jnp.dot(activ, w_fc2, precision=highest) + b_fc2)
    return middle + modul[5] * branch_mlp

def forward(tokens, cond, w_qkv, b_qv, w_proj, b_proj, w_fc1, b_fc1, w_fc2, b_fc2, w_ada, b_ada):
    silu_cond = low(jax.nn.silu(cond))
    bias_three = jnp.stack([b_qv[0], jnp.zeros_like(b_qv[0]), b_qv[1]])
    checked = jax.checkpoint(latent_block)

    def step(carry, pair):
        latent_rows, latent_cond = pair
        return (carry, checked(latent_rows, latent_cond, w_qkv, bias_three, w_proj, b_proj, w_fc1, b_fc1, w_fc2, b_fc2, w_ada, b_ada))
    _, outputs = lax.scan(step, jnp.zeros((), jnp.float32), (tokens.reshape(-1, LEN, D), silu_cond))
    return outputs.reshape(-1, D)

def reference(tokens, cond, cotangent, w_qkv, b_qv, w_proj, b_proj, w_fc1, b_fc1, w_fc2, b_fc2, w_ada, b_ada):
    primals = [arr.astype(jnp.float32) for arr in (tokens, cond, w_qkv, b_qv, w_proj, b_proj, w_fc1, b_fc1, w_fc2, b_fc2, w_ada, b_ada)]
    block_out, backward = jax.vjp(forward, *primals)
    grads = backward(cotangent.astype(jnp.float32))
    return (block_out.astype(jnp.bfloat16), grads[0].astype(jnp.bfloat16), grads[1], grads[2], grads[3], grads[4], grads[5], grads[6], grads[7], grads[8], grads[9], grads[10], grads[11])
```

```python
import math
from functools import partial

import jax
import jax.numpy as jnp
from jax import lax
from jax.experimental import pallas as pl
from jax.experimental.pallas import tpu as pltpu
from jax.sharding import PartitionSpec as P

HEAD_DIM = 64
LEN = 1024
PAIR = 2 * HEAD_DIM

norm_eps = 1e-06
highest = lax.Precision.HIGHEST
f32 = jnp.float32
bf16 = jnp.bfloat16

score_scale = HEAD_DIM ** (-0.5)
log2_scale = score_scale * math.log2(math.e)


def dot_nn(a, b):
    return lax.dot_general(a, b, (((1,), (0,)), ((), ())), preferred_element_type=f32)


def dot_nt(a, b):
    return lax.dot_general(a, b, (((1,), (1,)), ((), ())), preferred_element_type=f32)


def dot_tn(a, b):
    return lax.dot_general(a, b, (((0,), (0,)), ((), ())), preferred_element_type=f32)


def head_masks():
    lane = lax.broadcasted_iota(jnp.int32, (1, PAIR), 1)
    return [(lane < HEAD_DIM), (lane >= HEAD_DIM)]


def attend_kernel(step_rows, q_ref, k_ref, v_ref, o_ref, lse_ref):
    rows = q_ref.shape[0]
    masks = head_masks()
    keys = k_ref[...]
    values_t = v_ref[...].astype(f32).T.astype(bf16)
    sub = lax.broadcasted_iota(jnp.int32, (PAIR, 1), 0)
    for start in range(0, rows, step_rows):
        queries = q_ref[start : start + step_rows, :]
        out_t = []
        for head in range(2):
            q_head = jnp.where(masks[head], queries, jnp.zeros_like(queries))
            scores = dot_nt(keys, q_head) * log2_scale
            peak = jnp.max(scores, 0, keepdims=True)
            terms = jnp.exp2(scores - peak)
            total = jnp.sum(terms, 0, keepdims=True)
            out_t.append(dot_nn(values_t, terms.astype(bf16)) * (1.0 / total))
            lse_ref[0, head : head + 1, start : start + step_rows] = peak + jnp.log2(total)
        joined = jnp.where(sub < HEAD_DIM, out_t[0], out_t[1])
        o_ref[start : start + step_rows, :] = joined.T.astype(bf16)


def attend(qkv, local_width):
    rows = qkv.shape[0]
    pairs = local_width // PAIR
    heads = local_width // HEAD_DIM
    spec = [
        pl.BlockSpec((rows, PAIR), partial(lambda part, i: (0, part * pairs + i), part))
        for part in range(3)
    ]
    return pl.pallas_call(
        partial(attend_kernel, 256),
        grid=(pairs,),
        in_specs=spec,
        out_specs=[
            pl.BlockSpec((rows, PAIR), lambda i: (0, i)),
            pl.BlockSpec((1, 2, rows), lambda i: (i, 0, 0)),
        ],
        out_shape=[
            jax.ShapeDtypeStruct((rows, local_width), bf16),
            jax.ShapeDtypeStruct((pairs, 2, rows), f32),
        ],
        compiler_params=pltpu.CompilerParams(vmem_limit_bytes=48 * 1024 * 1024),
        cost_estimate=pl.CostEstimate(
            flops=4 * heads * rows * rows * 256,
            bytes_accessed=rows * local_width * 8,
            transcendentals=heads * rows * rows,
        ),
        name="attend",
    )(qkv, qkv, qkv)


def attend_back_kernel(step_rows, q_ref, k_ref, v_ref, do_ref, lse_ref, dqkv_ref):
    rows = q_ref.shape[0]
    masks = head_masks()
    keys = k_ref[...]
    values = v_ref[...]
    sub = lax.broadcasted_iota(jnp.int32, (PAIR, 1), 0)
    keys_t = keys.astype(f32).T.astype(bf16)
    d_keys = jnp.zeros((rows, PAIR), f32)
    d_values = jnp.zeros((rows, PAIR), f32)
    for start in range(0, rows, step_rows):
        queries = q_ref[start : start + step_rows, :]
        d_out = do_ref[start : start + step_rows, :]
        dq_t = []
        for head in range(2):
            q_head = jnp.where(masks[head], queries, jnp.zeros_like(queries))
            do_head = jnp.where(masks[head], d_out, jnp.zeros_like(d_out))
            lse = lse_ref[0, head : head + 1, start : start + step_rows]
            probs = jnp.exp2(dot_nt(keys, q_head) * log2_scale - lse)
            d_probs = dot_nt(values, do_head)
            weighted = probs * d_probs
            row_dot = jnp.sum(weighted, 0, keepdims=True)
            d_scores = (weighted - probs * row_dot).astype(bf16)
            d_values = d_values + dot_nn(probs.astype(bf16), do_head)
            d_keys = d_keys + dot_nn(d_scores, q_head)
            dq_t.append(dot_nn(keys_t, d_scores))
        joined = jnp.where(sub < HEAD_DIM, dq_t[0], dq_t[1])
        dqkv_ref[0, start : start + step_rows, :] = (joined.T * score_scale).astype(bf16)
    dqkv_ref[1] = (d_keys * score_scale).astype(bf16)
    dqkv_ref[2] = d_values.astype(bf16)


def attend_back(qkv, grad_heads, lse, local_width):
    rows = qkv.shape[0]
    pairs = local_width // PAIR
    heads = local_width // HEAD_DIM
    spec = [
        pl.BlockSpec((rows, PAIR), partial(lambda part, i: (0, part * pairs + i), part))
        for part in range(3)
    ]
    return pl.pallas_call(
        partial(attend_back_kernel, 256),
        grid=(pairs,),
        in_specs=spec
        + [
            pl.BlockSpec((rows, PAIR), lambda i: (0, i)),
            pl.BlockSpec((1, 2, rows), lambda i: (i, 0, 0)),
        ],
        out_specs=pl.BlockSpec((3, rows, PAIR), lambda i: (0, 0, i)),
        out_shape=jax.ShapeDtypeStruct((3, rows, local_width), bf16),
        compiler_params=pltpu.CompilerParams(vmem_limit_bytes=48 * 1024 * 1024),
        cost_estimate=pl.CostEstimate(
            flops=10 * heads * rows * rows * 256,
            bytes_accessed=rows * local_width * 14,
            transcendentals=heads * rows * rows,
        ),
        name="attend_back",
    )(qkv, qkv, qkv, grad_heads, lse)


def normalize(values):
    centred = values - jnp.mean(values, -1, keepdims=True)
    rstd = lax.rsqrt(jnp.mean(centred * centred, -1, keepdims=True) + norm_eps)
    return (centred * rstd, rstd)


def norm_back(grad_n, normed, rstd):
    first = jnp.mean(grad_n, -1, keepdims=True)
    second = jnp.mean(grad_n * normed, -1, keepdims=True)
    return rstd * (grad_n - first - normed * second)


def gelu_both(v):
    c = math.sqrt(2.0 / math.pi)
    sq = v * v
    th = jnp.tanh(c * v * (1.0 + 0.044715 * sq))
    half = 0.5 * (1.0 + th)
    slope = half + 0.5 * v * (1.0 - th * th) * c * (1.0 + 3 * 0.044715 * sq)
    return v * half, slope


def shift(x, axis, step):
    size = lax.axis_size(axis)
    return lax.ppermute(x, axis, [(i, (i + step) % size) for i in range(size)])


def xor_step(x, axis, bit):
    size = lax.axis_size(axis)
    return lax.ppermute(x, axis, [(i, i ^ bit) for i in range(size)])


def xor_gather(x, axis):
    size, bit = lax.axis_size(axis), 1
    out = x[None]
    while bit < size:
        out = jnp.concatenate([out, xor_step(out, axis, bit)], 0)
        bit *= 2
    return out


def xor_scatter_sum(x, axis):
    half = lax.axis_size(axis) // 2
    while half:
        x = x[:half] + xor_step(x[half:], axis, half)
        half //= 2
    return x[0]


def xor_sum(x, axis):
    size, bit = lax.axis_size(axis), 1
    while bit < size:
        x = x + xor_step(x, axis, bit)
        bit *= 2
    return x


def sort_xor(x, axis):
    size = lax.axis_size(axis)
    me = lax.axis_index(axis)
    order = jnp.arange(size, dtype=jnp.int32)
    pick = ((order[:, None] ^ me) == order[None, :]).astype(f32)
    flat = x.reshape(size, -1).astype(f32)
    return jnp.dot(pick, flat, precision=highest).reshape(x.shape)


def rel_gather(x, axis):
    return [x] + [shift(x, axis, s) for s in range(1, lax.axis_size(axis))]


def sort_rel(parts, axis):
    size = lax.axis_size(axis)
    me = lax.axis_index(axis)
    out = []
    for target in range(size):
        value = jnp.zeros_like(parts[0])
        for s in range(size):
            value = jnp.where(lax.rem(me - s + size, size) == target, parts[s], value)
        out.append(value)
    return out


def shards(
    tokens, cond, cotangent, w_qkv, b_qv, w_proj, b_proj, w_fc1, b_fc1, w_fc2, b_fc2, w_ada, b_ada
):
    tensor_size = lax.axis_size("tensor")
    dp_size = lax.axis_size("dp")
    tensor_pos = lax.axis_index("tensor")
    dp_pos = lax.axis_index("dp")
    row_count, width = tokens.shape
    group_rows = row_count * tensor_size
    depth = w_qkv.shape[0]
    local_width = w_qkv.shape[2]
    hidden = w_fc1.shape[1]
    assert cond.shape[0] == 1 and group_rows == LEN

    proj_t = w_proj.T
    proj_parts = rel_gather(proj_t, "tensor")
    attn_shard = jnp.concatenate([w_qkv.reshape(depth, 3 * local_width)] + proj_parts, 1)
    mlp_shard = jnp.concatenate([w_fc1, w_fc2.T], 1)
    attn_w = lax.all_gather(attn_shard, "dp", axis=0, tiled=True)
    mlp_w = lax.all_gather(mlp_shard, "dp", axis=0, tiled=True)
    qkv_w = attn_w[:, : 3 * local_width]
    proj_w = attn_w[:, 3 * local_width :]
    fc1_w = mlp_w[:, :hidden]
    fc2_w = mlp_w[:, hidden:]

    tok_parts = rel_gather(tokens, "tensor")
    vectors = jnp.concatenate(
        [b_qv.reshape(-1), b_proj, b_fc1, b_fc2, b_ada.reshape(-1)]
    )
    vec_size = vectors.shape[0]
    packed = jnp.concatenate([cond.reshape(-1)] + rel_gather(vectors, "tensor"))
    packed = xor_gather(packed, "dp")
    cond_all = packed[:, :width]
    vec_all = sort_xor(packed[:, width:], "dp").reshape(dp_size, tensor_size, vec_size)
    vec_sorted = sort_rel([vec_all[:, s] for s in range(tensor_size)], "tensor")
    own_vec = vec_all[:, 0]
    piece = b_proj.shape[0]
    n_fc1 = b_fc1.shape[0]
    at_proj = 2 * piece
    at_fc1 = at_proj + piece
    at_fc2 = at_fc1 + n_fc1
    at_ada = at_fc2 + piece
    qv_bias = own_vec[:, :at_proj].reshape(dp_size, 2, piece).transpose(1, 0, 2).reshape(2, local_width)
    fc1_bias = own_vec[:, at_fc1:at_fc2].reshape(hidden)
    ada_bias = (
        own_vec[:, at_ada:].reshape(dp_size, 6, piece).transpose(1, 0, 2).reshape(6, local_width)
    )
    proj_bias = jnp.concatenate([v[:, at_proj:at_fc1].reshape(-1) for v in vec_sorted])
    fc2_bias = jnp.concatenate([v[:, at_fc2:at_ada].reshape(-1) for v in vec_sorted])

    silu_all = jax.nn.silu(cond_all.astype(f32)).astype(bf16)
    silu_own = lax.dynamic_slice(silu_all, (0, dp_pos * depth), (dp_size, depth))
    ada_flat = w_ada.reshape(depth, 6 * local_width)
    mod_part = dot_nn(silu_own, ada_flat)
    mod_half = xor_scatter_sum(mod_part, "dp").reshape(6, local_width) + ada_bias
    modul = jnp.concatenate(sort_rel(rel_gather(mod_half, "tensor"), "tensor"), 1)
    shift_one, scale_one, gate_one, shift_two, scale_two, gate_two = [
        modul[k : k + 1] for k in range(6)
    ]

    inputs = jnp.concatenate(tok_parts, 0).astype(f32)
    normed_one, rstd_one = normalize(inputs)
    hidden_one = (normed_one * (1.0 + scale_one) + shift_one).astype(bf16)
    bias_three = jnp.concatenate([qv_bias[0], jnp.zeros_like(qv_bias[0]), qv_bias[1]])
    qkv = (dot_nn(hidden_one, qkv_w) + bias_three).astype(bf16)
    heads_out, lse = attend(qkv, local_width)
    heads_parts = [
        jnp.roll(part, s * row_count, 0)
        for s, part in enumerate(rel_gather(heads_out, "tensor"))
    ]
    heads_all = jnp.concatenate(heads_parts, 1)
    branch_attn = dot_nt(heads_all, proj_w) + proj_bias
    middle = inputs + gate_one * branch_attn
    normed_two, rstd_two = normalize(middle)
    hidden_two = (normed_two * (1.0 + scale_two) + shift_two).astype(bf16)

    cot_all = jnp.concatenate(rel_gather(cotangent, "tensor"), 0)
    grad_m = (gate_two * cot_all.astype(f32)).astype(bf16)
    grad_act = dot_nn(grad_m, fc2_w)
    pre_act = dot_nn(hidden_two, fc1_w) + fc1_bias
    activ, slope = gelu_both(pre_act)
    activ = activ.astype(bf16)
    grad_pre = (grad_act * slope).astype(bf16)

    def to_owners(rows_full, weight):
        own = dot_nt(rows_full[:row_count], weight)
        for s in range(1, tensor_size):
            part = dot_nt(rows_full[s * row_count : (s + 1) * row_count], weight).astype(bf16)
            own = own + shift(part, "tensor", -s).astype(f32)
        return own

    grad_hidden_two = to_owners(grad_pre, fc1_w)
    branch_mlp = dot_nt(activ, fc2_w)
    mlp_own = branch_mlp[:row_count]
    for s in range(1, tensor_size):
        part = branch_mlp[s * row_count : (s + 1) * row_count].astype(bf16)
        mlp_own = mlp_own + shift(part, "tensor", -s).astype(f32)
    branch_mlp = mlp_own + fc2_bias
    grad_out = cotangent.astype(f32)
    mid_own = middle[:row_count]
    block_out = (mid_own + gate_two * branch_mlp).astype(bf16)
    mlp_grads = jnp.concatenate(
        [dot_tn(hidden_two, grad_pre).astype(bf16), dot_tn(grad_m, activ).astype(bf16)], 1
    )
    mlp_grads = lax.psum_scatter(mlp_grads, "dp", scatter_dimension=0, tiled=True)

    n2, r2 = normed_two[:row_count], rstd_two[:row_count]
    grad_mid = grad_out + norm_back(grad_hidden_two * (1.0 + scale_two), n2, r2)
    grad_a = (gate_one * grad_mid).astype(bf16)
    grad_heads_all = dot_nn(grad_a, proj_w).astype(bf16)
    grad_heads = [grad_heads_all[:, :local_width]]
    for j in range(1, tensor_size):
        s = tensor_size - j
        part = grad_heads_all[:, s * local_width : (s + 1) * local_width]
        grad_heads.append(shift(part, "tensor", -s))
    grad_heads = jnp.concatenate(grad_heads, 0)
    grad_a_rows = jnp.concatenate(rel_gather(grad_a, "tensor"), 0)
    grad_proj = dot_tn(grad_a_rows, heads_out).astype(bf16)
    dqkv = attend_back(qkv, grad_heads, lse, local_width)
    dqkv = jnp.concatenate([dqkv[0], dqkv[1], dqkv[2]], 1)
    grad_hidden_one = to_owners(dqkv, qkv_w)
    attn_grads = jnp.concatenate([dot_tn(hidden_one, dqkv).astype(bf16), grad_proj], 1)
    attn_grads = lax.psum_scatter(attn_grads, "dp", scatter_dimension=0, tiled=True)

    n1, r1 = normed_one[:row_count], rstd_one[:row_count]
    grad_tokens = (
        grad_mid + norm_back(grad_hidden_one * (1.0 + scale_one), n1, r1)
    ).astype(bf16)

    def row_sum(v):
        return jnp.sum(v, 0, dtype=f32)

    grad_mod = jnp.stack(
        [
            row_sum(grad_hidden_one),
            row_sum(grad_hidden_one * n1),
            row_sum(grad_mid * branch_attn[:row_count]),
            row_sum(grad_hidden_two),
            row_sum(grad_hidden_two * n2),
            row_sum(grad_out * branch_mlp),
        ]
    )

    def cols_of(values, owner):
        return lax.dynamic_slice_in_dim(values, owner * local_width, local_width, values.ndim - 1)

    grad_mod_own = cols_of(grad_mod, tensor_pos)
    for s in range(1, tensor_size):
        owner = lax.rem(tensor_pos - s + tensor_size, tensor_size)
        grad_mod_own = grad_mod_own + shift(cols_of(grad_mod, owner), "tensor", -s)
    grad_mod_all = xor_gather(grad_mod_own.astype(bf16).reshape(6 * local_width), "dp")
    grad_ada = dot_tn(silu_own, grad_mod_all).reshape(depth, 6, local_width)
    ada_sum = jnp.sum(grad_mod_all, 0, dtype=f32).reshape(6, local_width)
    grad_ada_bias = lax.dynamic_slice_in_dim(ada_sum, dp_pos * piece, piece, 1)
    grad_silu_part = dot_nt(grad_mod_all, ada_flat)
    for s in range(1, tensor_size):
        grad_silu_part = grad_silu_part + shift(dot_nt(grad_mod_all, ada_flat), "tensor", s)
    grad_silu_all = xor_gather(grad_silu_part, "dp")
    order = jnp.arange(dp_size, dtype=jnp.int32)
    mine = (order[:, None] == order[None, :]).astype(f32)
    grad_silu = sort_xor(jnp.sum(grad_silu_all * mine[:, :, None], 1), "dp").reshape(1, width)
    _, silu_back = jax.vjp(jax.nn.silu, cond.astype(f32))
    grad_cond = silu_back(grad_silu)[0]

    grad_vec = jnp.concatenate(
        [
            row_sum(dqkv[:, :local_width].astype(f32)),
            row_sum(dqkv[:, 2 * local_width :].astype(f32)),
            cols_of(row_sum(grad_a_rows.astype(f32)), tensor_pos),
            row_sum(grad_pre.astype(f32)),
            cols_of(row_sum(grad_m.astype(f32)), tensor_pos),
        ]
    )
    grad_vec = xor_sum(grad_vec, "dp")

    def own_piece(start, size):
        return lax.dynamic_slice_in_dim(grad_vec, start + dp_pos * size, size, 0)

    grad_qv_bias = jnp.stack([own_piece(0, piece), own_piece(local_width, piece)])
    grad_proj_bias = own_piece(2 * local_width, piece)
    grad_fc1_bias = own_piece(3 * local_width, n_fc1)
    grad_fc2_bias = own_piece(3 * local_width + hidden, piece)

    attn_grads = attn_grads.astype(f32)
    mlp_grads = mlp_grads.astype(f32)
    return (
        block_out,
        grad_tokens,
        grad_cond,
        attn_grads[:, : 3 * local_width].reshape(depth, 3, local_width),
        grad_qv_bias,
        attn_grads[:, 3 * local_width :].T,
        grad_proj_bias,
        mlp_grads[:, :hidden],
        grad_fc1_bias,
        mlp_grads[:, hidden:].T,
        grad_fc2_bias,
        grad_ada,
        grad_ada_bias,
    )


def solution(mesh):
    placed = (
        P(("dp", "tensor"), None),
        P("dp", None),
        P(("dp", "tensor"), None),
        P("dp", None, "tensor"),
        P(None, ("tensor", "dp")),
        P("tensor", "dp"),
        P(("tensor", "dp")),
        P("dp", "tensor"),
        P(("tensor", "dp")),
        P("tensor", "dp"),
        P(("tensor", "dp")),
        P("dp", None, "tensor"),
        P(None, ("tensor", "dp")),
    )
    return jax.shard_map(
        shards,
        mesh=mesh,
        in_specs=placed,
        out_specs=(
            P(("dp", "tensor"), None),
            P(("dp", "tensor"), None),
            P("dp", None),
            P("dp", None, "tensor"),
            P(None, ("tensor", "dp")),
            P("tensor", "dp"),
            P(("tensor", "dp")),
            P("dp", "tensor"),
            P(("tensor", "dp")),
            P("tensor", "dp"),
            P(("tensor", "dp")),
            P("dp", None, "tensor"),
            P(None, ("tensor", "dp")),
        ),
        check_vma=False,
    )
```

```python
import math
from functools import partial

import jax
import jax.numpy as jnp
from jax import lax
from jax.experimental import pallas as pl
from jax.experimental.pallas import tpu as pltpu
from jax.sharding import PartitionSpec as P

HEAD_DIM = 64
LEN = 1024
PAIR = 2 * HEAD_DIM

norm_eps = 1e-06
highest = lax.Precision.HIGHEST
f32 = jnp.float32
bf16 = jnp.bfloat16

score_scale = HEAD_DIM ** (-0.5)
log2_scale = score_scale * math.log2(math.e)


MIB = 1024 * 1024


def dot_nn(a, b):
    return lax.dot_general(a, b, (((1,), (0,)), ((), ())), preferred_element_type=f32)


def dot_nt(a, b):
    return lax.dot_general(a, b, (((1,), (1,)), ((), ())), preferred_element_type=f32)


def dot_tn(a, b):
    return lax.dot_general(a, b, (((0,), (0,)), ((), ())), preferred_element_type=f32)


def head_masks():
    lane = lax.broadcasted_iota(jnp.int32, (1, PAIR), 1)
    return [(lane < HEAD_DIM), (lane >= HEAD_DIM)]


def attend_kernel(step_rows, q_ref, k_ref, v_ref, o_ref, lse_ref):
    rows = q_ref.shape[0]
    masks = head_masks()
    keys = k_ref[...]
    values_t = v_ref[...].astype(f32).T.astype(bf16)
    sub = lax.broadcasted_iota(jnp.int32, (PAIR, 1), 0)
    for start in range(0, rows, step_rows):
        queries = q_ref[start : start + step_rows, :]
        out_t = []
        for head in range(2):
            q_head = jnp.where(masks[head], queries, jnp.zeros_like(queries))
            scores = dot_nt(keys, q_head) * log2_scale
            peak = jnp.max(scores, 0, keepdims=True)
            terms = jnp.exp2(scores - peak)
            total = jnp.sum(terms, 0, keepdims=True)
            out_t.append(dot_nn(values_t, terms.astype(bf16)) * (1.0 / total))
            lse_ref[0, head : head + 1, start : start + step_rows] = peak + jnp.log2(total)
        joined = jnp.where(sub < HEAD_DIM, out_t[0], out_t[1])
        o_ref[start : start + step_rows, :] = joined.T.astype(bf16)


def attend(qkv, local_width):
    rows = qkv.shape[0]
    pairs = local_width // PAIR
    heads = local_width // HEAD_DIM
    spec = [
        pl.BlockSpec((rows, PAIR), partial(lambda part, i: (0, part * pairs + i), part))
        for part in range(3)
    ]
    return pl.pallas_call(
        partial(attend_kernel, 256),
        grid=(pairs,),
        in_specs=spec,
        out_specs=[
            pl.BlockSpec((rows, PAIR), lambda i: (0, i)),
            pl.BlockSpec((1, 2, rows), lambda i: (i, 0, 0)),
        ],
        out_shape=[
            jax.ShapeDtypeStruct((rows, local_width), bf16),
            jax.ShapeDtypeStruct((pairs, 2, rows), f32),
        ],
        compiler_params=pltpu.CompilerParams(vmem_limit_bytes=28 * MIB),
        cost_estimate=pl.CostEstimate(
            flops=4 * heads * rows * rows * 256,
            bytes_accessed=rows * local_width * 8,
            transcendentals=heads * rows * rows,
        ),
        name="attend",
    )(qkv, qkv, qkv)


def attend_back_kernel(step_rows, q_ref, k_ref, v_ref, do_ref, lse_ref, dqkv_ref):
    rows = q_ref.shape[0]
    masks = head_masks()
    keys = k_ref[...]
    values = v_ref[...]
    sub = lax.broadcasted_iota(jnp.int32, (PAIR, 1), 0)
    keys_t = keys.astype(f32).T.astype(bf16)
    d_keys = jnp.zeros((rows, PAIR), f32)
    d_values = jnp.zeros((rows, PAIR), f32)
    for start in range(0, rows, step_rows):
        queries = q_ref[start : start + step_rows, :]
        d_out = do_ref[start : start + step_rows, :]
        dq_t = []
        for head in range(2):
            q_head = jnp.where(masks[head], queries, jnp.zeros_like(queries))
            do_head = jnp.where(masks[head], d_out, jnp.zeros_like(d_out))
            lse = lse_ref[0, head : head + 1, start : start + step_rows]
            probs = jnp.exp2(dot_nt(keys, q_head) * log2_scale - lse)
            d_probs = dot_nt(values, do_head)
            weighted = probs * d_probs
            row_dot = jnp.sum(weighted, 0, keepdims=True)
            d_scores = (weighted - probs * row_dot).astype(bf16)
            d_values = d_values + dot_nn(probs.astype(bf16), do_head)
            d_keys = d_keys + dot_nn(d_scores, q_head)
            dq_t.append(dot_nn(keys_t, d_scores))
        joined = jnp.where(sub < HEAD_DIM, dq_t[0], dq_t[1])
        dqkv_ref[0, start : start + step_rows, :] = (joined.T * score_scale).astype(bf16)
    dqkv_ref[1] = (d_keys * score_scale).astype(bf16)
    dqkv_ref[2] = d_values.astype(bf16)


def attend_back(qkv, grad_heads, lse, local_width):
    rows = qkv.shape[0]
    pairs = local_width // PAIR
    heads = local_width // HEAD_DIM
    spec = [
        pl.BlockSpec((rows, PAIR), partial(lambda part, i: (0, part * pairs + i), part))
        for part in range(3)
    ]
    return pl.pallas_call(
        partial(attend_back_kernel, 256),
        grid=(pairs,),
        in_specs=spec
        + [
            pl.BlockSpec((rows, PAIR), lambda i: (0, i)),
            pl.BlockSpec((1, 2, rows), lambda i: (i, 0, 0)),
        ],
        out_specs=pl.BlockSpec((3, rows, PAIR), lambda i: (0, 0, i)),
        out_shape=jax.ShapeDtypeStruct((3, rows, local_width), bf16),
        compiler_params=pltpu.CompilerParams(vmem_limit_bytes=28 * MIB),
        cost_estimate=pl.CostEstimate(
            flops=10 * heads * rows * rows * 256,
            bytes_accessed=rows * local_width * 14,
            transcendentals=heads * rows * rows,
        ),
        name="attend_back",
    )(qkv, qkv, qkv, grad_heads, lse)


def normalize(values):
    mean = jnp.mean(values, -1, keepdims=True)
    centred = values - mean
    rstd = lax.rsqrt(jnp.mean(centred * centred, -1, keepdims=True) + norm_eps)
    return (centred * rstd, mean, rstd)


def norm_back(grad_n, normed, rstd):
    first = jnp.mean(grad_n, -1, keepdims=True)
    second = jnp.mean(grad_n * normed, -1, keepdims=True)
    return rstd * (grad_n - first - normed * second)


def gelu_both(v):
    c = math.sqrt(2.0 / math.pi)
    sq = v * v
    half = 0.5 + 0.5 * jnp.tanh(v * (c + c * 0.044715 * sq))
    act = v * half
    slope = half + act * (1.0 - half) * (2 * c + 6 * c * 0.044715 * sq)
    return act, slope


def full_spec(shape):
    return pl.BlockSpec(shape, lambda *_: (0,) * len(shape))


def mlp_kernel(
    own_rows, step_rows, h_ref, dm_ref, w1_ref, w2_ref, b1_ref,
    act_ref, dpre_ref, db_ref, own_ref, rest_ref, acc_ref,
):
    j = pl.program_id(0)

    @pl.when(j == 0)
    def _():
        acc_ref[...] = jnp.zeros_like(acc_ref)

    rows = h_ref.shape[0]
    w1, w2, b1 = w1_ref[...], w2_ref[...], b1_ref[...]
    total = jnp.zeros((1, w1.shape[1]), f32)
    for start in range(0, rows, step_rows):
        part = slice(start, start + step_rows)
        pre = dot_nn(h_ref[part, :], w1) + b1
        d_act = dot_nn(dm_ref[part, :], w2)
        act, slope = gelu_both(pre)
        d_pre = d_act * slope
        d_low = d_pre.astype(bf16)
        act_ref[part, :] = act.astype(bf16)
        dpre_ref[part, :] = d_low
        total = total + jnp.sum(d_pre, 0, keepdims=True)
        acc_ref[part, :] += dot_nt(d_low, w1)
    db_ref[...] = total

    @pl.when(j == pl.num_programs(0) - 1)
    def _():
        own_ref[...] = acc_ref[:own_rows, :]
        rest_ref[...] = acc_ref[own_rows:, :].astype(bf16)


def mlp_both(hidden_two, grad_m, mlp_w, bias, own_rows):
    rows, width = hidden_two.shape
    hidden = mlp_w.shape[1] // 2
    block = min(512, hidden)
    steps = hidden // block
    return pl.pallas_call(
        partial(mlp_kernel, own_rows, 256),
        grid=(steps,),
        in_specs=[
            full_spec((rows, width)),
            full_spec((rows, width)),
            pl.BlockSpec((width, block), lambda j: (0, j)),
            pl.BlockSpec((width, block), lambda j: (0, steps + j)),
            pl.BlockSpec((1, block), lambda j: (0, j)),
        ],
        out_specs=[
            pl.BlockSpec((rows, block), lambda j: (0, j)),
            pl.BlockSpec((rows, block), lambda j: (0, j)),
            pl.BlockSpec((1, block), lambda j: (0, j)),
            full_spec((own_rows, width)),
            full_spec((rows - own_rows, width)),
        ],
        out_shape=[
            jax.ShapeDtypeStruct((rows, hidden), bf16),
            jax.ShapeDtypeStruct((rows, hidden), bf16),
            jax.ShapeDtypeStruct((1, hidden), f32),
            jax.ShapeDtypeStruct((own_rows, width), f32),
            jax.ShapeDtypeStruct((rows - own_rows, width), bf16),
        ],
        scratch_shapes=[pltpu.VMEM((rows, width), f32)],
        compiler_params=pltpu.CompilerParams(vmem_limit_bytes=48 * MIB),
        cost_estimate=pl.CostEstimate(
            flops=6 * rows * width * hidden,
            bytes_accessed=4 * rows * hidden + 6 * width * hidden + 8 * rows * width,
            transcendentals=rows * hidden,
        ),
        name="mlp_both",
    )(hidden_two, grad_m, mlp_w, mlp_w, bias)


def transpose_low(value):
    return value.astype(f32).T.astype(bf16)


def mlp_grads_kernel(own_rows, half, h_ref, dm_ref, dpre_ref, act_ref, w2_ref, cot_ref, grad_ref, own_ref, rest_ref, sum_ref, h_t, dm_t, acc_ref):
    j = pl.program_id(0)

    @pl.when(j == 0)
    def _():
        h_t[...] = transpose_low(h_ref[...])
        dm_t[...] = transpose_low(dm_ref[...])
        acc_ref[...] = jnp.zeros_like(acc_ref)

    @pl.when(j < half)
    def _():
        grad_ref[...] = dot_nn(h_t[...], dpre_ref[...]).astype(bf16)

    @pl.when(j >= half)
    def _():
        grad_ref[...] = dot_nn(dm_t[...], act_ref[...]).astype(bf16)
        acc_ref[...] += dot_nt(act_ref[...], w2_ref[...])

    @pl.when(j == 2 * half - 1)
    def _():
        own_ref[...] = acc_ref[:own_rows, :]
        rest_ref[...] = acc_ref[own_rows:, :].astype(bf16)
        sum_ref[...] = jnp.sum(acc_ref[...] * cot_ref[...].astype(f32), 0, keepdims=True)


def mlp_weight_grads(hidden_two, grad_m, grad_pre, activ, mlp_w, cot_all, own_rows):
    rows, width = hidden_two.shape
    hidden = mlp_w.shape[1] // 2
    block = min(512, hidden)
    half = hidden // block
    return pl.pallas_call(
        partial(mlp_grads_kernel, own_rows, half),
        grid=(2 * half,),
        in_specs=[
            full_spec((rows, width)),
            full_spec((rows, width)),
            pl.BlockSpec((rows, block), lambda j: (0, jnp.minimum(j, half - 1))),
            pl.BlockSpec((rows, block), lambda j: (0, jnp.maximum(j - half, 0))),
            pl.BlockSpec((width, block), lambda j: (0, half + jnp.maximum(j - half, 0))),
            full_spec((rows, width)),
        ],
        out_specs=[
            pl.BlockSpec((width, block), lambda j: (0, j)),
            full_spec((own_rows, width)),
            full_spec((rows - own_rows, width)),
            full_spec((1, width)),
        ],
        out_shape=[
            jax.ShapeDtypeStruct((width, 2 * hidden), bf16),
            jax.ShapeDtypeStruct((own_rows, width), f32),
            jax.ShapeDtypeStruct((rows - own_rows, width), bf16),
            jax.ShapeDtypeStruct((1, width), f32),
        ],
        scratch_shapes=[
            pltpu.VMEM((width, rows), bf16),
            pltpu.VMEM((width, rows), bf16),
            pltpu.VMEM((rows, width), f32),
        ],
        compiler_params=pltpu.CompilerParams(vmem_limit_bytes=48 * MIB),
        cost_estimate=pl.CostEstimate(
            flops=6 * rows * width * hidden,
            bytes_accessed=4 * rows * hidden + 6 * width * hidden + 8 * rows * width,
            transcendentals=0,
        ),
        name="mlp_weight_grads",
    )(hidden_two, grad_m, grad_pre, activ, mlp_w, cot_all)


def middle_kernel(own_steps, pieces, *refs):
    heads = [ref[...] for ref in refs[:pieces]]
    w_ref, x_ref, cot_ref, mod_ref = refs[pieces : pieces + 4]
    h_ref, dm_ref, sum_ref, a_ref, x1_ref, mean_ref, rstd_ref = refs[pieces + 4 :]
    i = pl.program_id(0)
    branch = dot_nt(jnp.concatenate(heads, 1), w_ref[...]) + mod_ref[6:7, :]
    middle = x_ref[...].astype(f32) + mod_ref[2:3, :] * branch
    normed, mean, rstd = normalize(middle)
    h_ref[...] = (normed * (1.0 + mod_ref[4:5, :]) + mod_ref[3:4, :]).astype(bf16)
    low = (mod_ref[5:6, :] * cot_ref[...].astype(f32)).astype(bf16)
    dm_ref[...] = low
    total = jnp.sum(low.astype(f32), 0, keepdims=True)

    @pl.when(i == 0)
    def _():
        sum_ref[...] = total

    @pl.when(i > 0)
    def _():
        sum_ref[...] += total

    @pl.when(i < own_steps)
    def _():
        a_ref[...] = branch
        x1_ref[...] = middle
        mean_ref[...] = mean
        rstd_ref[...] = rstd


def middle_part(heads, weight, x_all, cot_all, modul, own_rows):
    rows, width = x_all.shape
    block = min(256, own_rows)
    steps, own_steps = rows // block, own_rows // block
    specs, arrays = [], []
    for s, parts in enumerate(heads):
        for part in parts:
            specs.append(
                pl.BlockSpec(
                    (block, part.shape[1]),
                    partial(lambda back, i: (lax.rem(i - back + steps, steps), 0), s * own_steps),
                )
            )
            arrays.append(part)
    row_spec = pl.BlockSpec((block, width), lambda i: (i, 0))
    own_spec = pl.BlockSpec((block, width), lambda i: (jnp.minimum(i, own_steps - 1), 0))
    one_spec = pl.BlockSpec((block, 1), lambda i: (jnp.minimum(i, own_steps - 1), 0))
    return pl.pallas_call(
        partial(middle_kernel, own_steps, len(arrays)),
        grid=(steps,),
        in_specs=specs
        + [full_spec((width, width)), row_spec, row_spec, full_spec(modul.shape)],
        out_specs=[row_spec, row_spec, full_spec((1, width)), own_spec, own_spec, one_spec, one_spec],
        out_shape=[
            jax.ShapeDtypeStruct((rows, width), bf16),
            jax.ShapeDtypeStruct((rows, width), bf16),
            jax.ShapeDtypeStruct((1, width), f32),
            jax.ShapeDtypeStruct((own_rows, width), f32),
            jax.ShapeDtypeStruct((own_rows, width), f32),
            jax.ShapeDtypeStruct((own_rows, 1), f32),
            jax.ShapeDtypeStruct((own_rows, 1), f32),
        ],
        compiler_params=pltpu.CompilerParams(vmem_limit_bytes=40 * MIB),
        cost_estimate=pl.CostEstimate(
            flops=2 * rows * width * width,
            bytes_accessed=12 * rows * width + 8 * own_rows * width,
            transcendentals=rows,
        ),
        name="middle_part",
    )(*arrays, weight, x_all, cot_all, modul)


def middle_back_kernel(others, pieces, own_ref, *refs):
    arrived = refs[:others]
    cot_ref, x1_ref, a_ref, mean_ref, rstd_ref, mod_ref, w_ref = refs[others : others + 7]
    mid_ref, da_ref, sums_ref = refs[others + 7 : others + 10]
    head_refs = refs[others + 10 :]
    grad_h = own_ref[...]
    for ref in arrived:
        grad_h = grad_h + ref[...].astype(f32)
    normed = (x1_ref[...] - mean_ref[...]) * rstd_ref[...]
    grad_mid = cot_ref[...].astype(f32) + norm_back(
        grad_h * (1.0 + mod_ref[4:5, :]), normed, rstd_ref[...]
    )
    grad_a = (mod_ref[2:3, :] * grad_mid).astype(bf16)
    mid_ref[...] = grad_mid
    da_ref[...] = grad_a
    sums = jnp.concatenate(
        [
            jnp.sum(grad_mid * a_ref[...], 0, keepdims=True),
            jnp.sum(grad_h, 0, keepdims=True),
            jnp.sum(grad_h * normed, 0, keepdims=True),
        ]
    )
    i = pl.program_id(0)

    @pl.when(i == 0)
    def _():
        sums_ref[...] = sums

    @pl.when(i > 0)
    def _():
        sums_ref[...] += sums

    grad_heads = dot_nn(grad_a, w_ref[...]).astype(bf16)
    columns = head_refs[0].shape[1]
    for p in range(pieces):
        head_refs[p][...] = grad_heads[:, p * columns : (p + 1) * columns]


def middle_back(own, arrived, cot, x1, branch, mean, rstd, modul, weight, columns):
    rows, width = own.shape
    block = min(256, rows)
    pieces = width // columns
    row_spec = pl.BlockSpec((block, width), lambda i: (i, 0))
    one_spec = pl.BlockSpec((block, 1), lambda i: (i, 0))
    return pl.pallas_call(
        partial(middle_back_kernel, len(arrived), pieces),
        grid=(rows // block,),
        in_specs=[row_spec] * (len(arrived) + 4)
        + [one_spec, one_spec, full_spec(modul.shape), full_spec((width, width))],
        out_specs=[row_spec, row_spec, full_spec((3, width))]
        + [pl.BlockSpec((block, columns), lambda i: (i, 0))] * pieces,
        out_shape=[
            jax.ShapeDtypeStruct((rows, width), f32),
            jax.ShapeDtypeStruct((rows, width), bf16),
            jax.ShapeDtypeStruct((3, width), f32),
        ]
        + [jax.ShapeDtypeStruct((rows, columns), bf16)] * pieces,
        compiler_params=pltpu.CompilerParams(vmem_limit_bytes=40 * MIB),
        cost_estimate=pl.CostEstimate(
            flops=2 * rows * width * width, bytes_accessed=28 * rows * width, transcendentals=0
        ),
        name="middle_back",
    )(own, *arrived, cot, x1, branch, mean, rstd, modul, weight)


def col_grads_kernel(count, depth, arrays, core_ref, left_ref, *refs):
    keep_ref, send_ref = refs[arrays:]
    left_t = transpose_low(left_ref[...])
    core = core_ref[0]
    at = 0
    for ref in refs[:arrays]:
        for p in range(ref.shape[0]):
            columns = slice(at, at + ref.shape[2])
            result = dot_nn(left_t, ref[p])
            for i in range(count // 2):
                low = result[2 * i * depth : (2 * i + 1) * depth]
                high = result[(2 * i + 1) * depth : (2 * i + 2) * depth]
                rows = slice(i * depth, (i + 1) * depth)
                keep_ref[rows, columns] = jnp.where(core == 0, low, high).astype(bf16)
                send_ref[rows, columns] = jnp.where(core == 0, high, low).astype(bf16)
            at += ref.shape[2]


def col_grads(left, rights, core, depth):
    rows, width = left.shape
    columns = sum(right.shape[0] * right.shape[2] for right in rights)
    out = jax.ShapeDtypeStruct((width // 2, columns), bf16)
    vmem = pl.BlockSpec(memory_space=pltpu.VMEM)
    return pl.pallas_call(
        partial(col_grads_kernel, width // depth, depth, len(rights)),
        in_specs=[pl.BlockSpec(memory_space=pltpu.SMEM)] + [vmem] * (1 + len(rights)),
        out_specs=[vmem, vmem],
        out_shape=[out, out],
        compiler_params=pltpu.CompilerParams(vmem_limit_bytes=40 * MIB),
        cost_estimate=pl.CostEstimate(
            flops=2 * rows * width * columns,
            bytes_accessed=2 * rows * width + 4 * rows * columns,
            transcendentals=0,
        ),
        name="col_grads",
    )(core, left, *rights)


def hidden_back_kernel(own_rows, groups, *refs):
    x_ref = refs[0]
    grads = refs[1 : 1 + groups]
    weights = refs[1 + groups : 1 + 2 * groups]
    own_ref, rest_ref, sums_ref, acc_ref = refs[1 + 2 * groups :]
    j = pl.program_id(0)
    part = dot_nt(grads[0][0], weights[0][...])
    for g in range(1, groups):
        part = part + dot_nt(grads[g][0], weights[g][...])

    @pl.when(j == 0)
    def _():
        acc_ref[...] = part

    @pl.when(j > 0)
    def _():
        acc_ref[...] += part

    @pl.when(j == pl.num_programs(0) - 1)
    def _():
        total = acc_ref[...]
        normed, _, _ = normalize(x_ref[...].astype(f32))
        own_ref[...] = total[:own_rows]
        rest_ref[...] = total[own_rows:].astype(bf16)
        sums_ref[0:1, :] = jnp.sum(total, 0, keepdims=True)
        sums_ref[1:2, :] = jnp.sum(total * normed, 0, keepdims=True)


def hidden_back(x_all, grads, weight, first, own_rows):
    rows, width = x_all.shape
    groups = len(grads)
    columns = grads[0].shape[2]
    return pl.pallas_call(
        partial(hidden_back_kernel, own_rows, groups),
        grid=(3,),
        in_specs=[full_spec((rows, width))]
        + [pl.BlockSpec((1, rows, columns), lambda j: (j, 0, 0))] * groups
        + [
            pl.BlockSpec((width, columns), partial(lambda at, j: (0, at + j), first // columns + 3 * g))
            for g in range(groups)
        ],
        out_specs=[
            full_spec((own_rows, width)),
            full_spec((rows - own_rows, width)),
            full_spec((2, width)),
        ],
        out_shape=[
            jax.ShapeDtypeStruct((own_rows, width), f32),
            jax.ShapeDtypeStruct((rows - own_rows, width), bf16),
            jax.ShapeDtypeStruct((2, width), f32),
        ],
        scratch_shapes=[pltpu.VMEM((rows, width), f32)],
        compiler_params=pltpu.CompilerParams(vmem_limit_bytes=40 * MIB),
        cost_estimate=pl.CostEstimate(
            flops=6 * rows * width * columns * groups,
            bytes_accessed=4 * rows * width + 12 * rows * columns * groups,
            transcendentals=0,
        ),
        name="hidden_back",
    )(x_all, *grads, *([weight] * groups))


def shift(x, axis, step):
    size = lax.axis_size(axis)
    return lax.ppermute(x, axis, [(i, (i + step) % size) for i in range(size)])


def xor_step(x, axis, bit):
    size = lax.axis_size(axis)
    return lax.ppermute(x, axis, [(i, i ^ bit) for i in range(size)])


def bits_of(side_last):
    size = lax.axis_size("dp")
    bits = [1 << k for k in range(size.bit_length() - 1)]
    return bits[:1] + bits[2:] + bits[1:2] if side_last else bits


def xor_of(side_last):
    bits = bits_of(side_last)
    place = jnp.arange(1 << len(bits), dtype=jnp.int32)
    return sum(((place >> k) & 1) * bit for k, bit in enumerate(bits))


def xor_gather(x, side_last):
    out = x[None]
    for bit in bits_of(side_last):
        out = jnp.concatenate([out, xor_step(out, "dp", bit)], 0)
    return out


def xor_scatter_sum(x, side_last):
    half = x.shape[0] // 2
    for bit in reversed(bits_of(side_last)):
        x = x[:half] + xor_step(x[half:], "dp", bit)
        half //= 2
    return x[0]


def xor_sum(x, side_last):
    for bit in bits_of(side_last):
        x = x + xor_step(x, "dp", bit)
    return x


def sort_xor(x, side_last):
    size = lax.axis_size("dp")
    me = lax.axis_index("dp")
    order = jnp.arange(size, dtype=jnp.int32)
    pick = ((order[:, None] ^ me) == xor_of(side_last)[None, :]).astype(f32)
    flat = x.reshape(size, -1).astype(f32)
    return jnp.dot(pick, flat, precision=highest).reshape(x.shape)


def rel_gather(x, axis):
    return [x] + [shift(x, axis, s) for s in range(1, lax.axis_size(axis))]


def sort_rel(parts, axis):
    size = lax.axis_size(axis)
    me = lax.axis_index(axis)
    out = []
    for target in range(size):
        value = jnp.zeros_like(parts[0])
        for s in range(size):
            value = jnp.where(lax.rem(me - s + size, size) == target, parts[s], value)
        out.append(value)
    return out


def together(run, work, *args):
    shapes = jax.eval_shape(work, *args)
    empty = lambda *_: jax.tree.map(lambda v: jnp.zeros(v.shape, v.dtype), shapes)
    return lax.cond(run, work, empty, *args)


def dp_place():
    size, me = lax.axis_size("dp"), lax.axis_index("dp")
    return size // 4, me // 4, lax.rem(me // 2, 2), lax.rem(me, 2)


def after(value, *others):
    return lax.optimization_barrier((value,) + others)[0]


def far_shift(x, step):
    size = lax.axis_size("dp")
    return lax.ppermute(x, "dp", [(i, (i + 4 * step) % size) for i in range(size)])


def add_low(keep, arrived):
    return (keep.astype(f32) + arrived.astype(f32)).astype(bf16)


def side_split(total, depth):
    far_size, _, side, _ = dp_place()
    total = total.reshape(far_size, 2, depth, total.shape[1])
    keep = lax.dynamic_index_in_dim(total, side, 1, keepdims=False)
    return keep, lax.dynamic_index_in_dim(total, 1 - side, 1, keepdims=False)


def far_split(total):
    far_size, far, _, _ = dp_place()
    rows = [
        lax.dynamic_index_in_dim(total, lax.rem(far + s, far_size), 0, keepdims=False)
        for s in range(far_size)
    ]
    return rows[0], rows[1:]


def shards(
    tokens, cond, cotangent, w_qkv, b_qv, w_proj, b_proj, w_fc1, b_fc1, w_fc2, b_fc2, w_ada, b_ada
):
    tensor_size = lax.axis_size("tensor")
    dp_size = lax.axis_size("dp")
    tensor_pos = lax.axis_index("tensor")
    dp_pos = lax.axis_index("dp")
    row_count, width = tokens.shape
    group_rows = row_count * tensor_size
    depth = w_qkv.shape[0]
    local_width = w_qkv.shape[2]
    hidden = w_fc1.shape[1]
    pairs = local_width // PAIR
    groups = 2 if pairs % 2 == 0 else 1
    group_width = local_width // groups
    assert cond.shape[0] == 1 and group_rows == LEN

    def row_sum(v):
        return jnp.sum(v, 0, dtype=f32)

    def cols_of(values, owner):
        return lax.dynamic_slice_in_dim(values, owner * local_width, local_width, values.ndim - 1)

    proj_parts = rel_gather(w_proj.T, "tensor")
    qkv_parts = [
        w_qkv[:, :, g * group_width : (g + 1) * group_width].reshape(depth, 3 * group_width)
        for g in range(groups)
    ]
    attn_w = lax.all_gather(jnp.concatenate(proj_parts + qkv_parts, 1), "dp", axis=0, tiled=True)
    mlp_w = lax.all_gather(jnp.concatenate([w_fc1, w_fc2.T], 1), "dp", axis=0, tiled=True)
    tok_parts = rel_gather(tokens, "tensor")
    cot_all = jnp.concatenate(rel_gather(after(cotangent, *tok_parts), "tensor"), 0)
    core_one = lax.rem(dp_pos, 2).astype(jnp.int32).reshape(1)

    vectors = jnp.concatenate([b_qv.reshape(-1), b_fc1])
    packed = xor_gather(jnp.concatenate([cond.reshape(-1), vectors]), True)
    cond_all = packed[:, :width]
    own_vec = sort_xor(packed[:, width:], True)
    piece = b_proj.shape[0]
    n_fc1 = b_fc1.shape[0]
    qv_bias = own_vec[:, : 2 * piece].reshape(dp_size, 2, piece).transpose(1, 0, 2)
    qv_bias = qv_bias.reshape(2, local_width)
    fc1_bias = own_vec[:, 2 * piece :].reshape(1, hidden)

    silu_all = jax.nn.silu(cond_all.astype(f32)).astype(bf16)
    silu_own = lax.dynamic_slice(silu_all, (0, dp_pos * depth), (dp_size, depth))
    ada_flat = w_ada.reshape(depth, 6 * local_width)
    biases = jnp.concatenate([b_ada, b_proj[None], b_fc2[None]]).astype(f32)
    lane = lax.broadcasted_iota(jnp.int32, (1, local_width), 1)
    biases = jnp.where(lane // piece == dp_pos, jnp.tile(biases, (1, dp_size)), 0.0)
    mod_part = jnp.pad(dot_nn(silu_own, ada_flat), ((0, 0), (0, 2 * local_width)))
    mod_part = mod_part + biases.reshape(1, 8 * local_width)
    mod_half = xor_scatter_sum(mod_part, True).reshape(8, local_width)
    modul = jnp.concatenate(sort_rel(rel_gather(mod_half, "tensor"), "tensor"), 1)
    shift_one, scale_one, gate_one, shift_two, scale_two, gate_two, proj_bias, fc2_bias = [
        modul[k : k + 1] for k in range(8)
    ]

    x_all = jnp.concatenate(tok_parts, 0)
    inputs = x_all.astype(f32)
    normed_one, mean_one, rstd_one = normalize(inputs)
    hidden_one = (normed_one * (1.0 + scale_one) + shift_one).astype(bf16)
    hidden_one = lax.optimization_barrier(hidden_one)
    qkv, heads_out, lse, heads_other = [], [], [], []
    for g in range(groups):
        cols = slice(g * group_width, (g + 1) * group_width)
        bias = jnp.concatenate([qv_bias[0, cols], jnp.zeros((group_width,), f32), qv_bias[1, cols]])
        left = hidden_one if g == 0 else after(hidden_one, heads_out[-1])
        at = width + 3 * group_width * g
        qkv.append((dot_nn(left, attn_w[:, at : at + 3 * group_width]) + bias).astype(bf16))
        out, log_total = attend(qkv[g], group_width)
        heads_out.append(out)
        lse.append(log_total)
        heads_other.append([shift(out, "tensor", s) for s in range(1, tensor_size)])
    heads_rel = [heads_out] + [[v[s - 1] for v in heads_other] for s in range(1, tensor_size)]
    hidden_two, grad_m, dm_sum, branch_attn, middle, mean_two, rstd_two = middle_part(
        heads_rel, attn_w, x_all, cot_all, modul, row_count
    )

    activ, grad_pre, fc1_sum, own_two, rest_two = mlp_both(
        hidden_two, grad_m, mlp_w, fc1_bias, row_count
    )

    def owners_sum(own, rest):
        arrived = [
            shift(rest[(s - 1) * row_count : s * row_count], "tensor", -s)
            for s in range(1, tensor_size)
        ]
        return own, arrived

    def add_up(own, arrived):
        for part in arrived:
            own = own + part.astype(f32)
        return own

    run = dp_pos >= 0

    def weight_part(rest_two, *args):
        arrived = owners_sum(None, rest_two)[1]
        return arrived, mlp_weight_grads(*args, row_count)

    arrived_two, (mlp_grads, own_mlp, rest_mlp, mlp_sum) = together(
        run, weight_part, rest_two, hidden_two, grad_m, grad_pre, activ, mlp_w, cot_all
    )
    mlp_grads = lax.psum_scatter(mlp_grads, "dp", scatter_dimension=0, tiled=True)

    grad_out = cotangent.astype(f32)
    grad_mid, grad_a, sums_two, *grad_pieces = middle_back(
        own_two, arrived_two, cotangent, middle, branch_attn, mean_two, rstd_two, modul, attn_w, group_width
    )

    def heads_of(pieces, g):
        parts = [pieces[g]]
        for j in range(1, tensor_size):
            s = tensor_size - j
            parts.append(shift(pieces[s * groups + g], "tensor", -s))
        return jnp.concatenate(parts, 0)

    last = groups - 1
    grad_heads = heads_of(grad_pieces, 0)
    dqkv, early = [], []
    if last:

        def first_group(pieces, heads, qkv_g, lse_g, left):
            moved = heads_of(pieces, 1)
            grads = attend_back(qkv_g, heads, lse_g, group_width)
            return moved, grads, col_grads(left, [grads], core_one, depth)

        grad_heads, grads, early = together(
            run, first_group, grad_pieces, grad_heads, qkv[0], lse[0], hidden_one
        )
        dqkv.append(grads)

    def last_group(grad_a, early, heads, qkv_g, lse_g, before, x_all):
        grad_a_rows = jnp.concatenate(rel_gather(grad_a, "tensor"), 0)
        if early:
            early = add_low(early[0], xor_step(early[1], "dp", 1))
        grads = attend_back(qkv_g, heads, lse_g, group_width)
        back = hidden_back(x_all, before + [grads], attn_w, width, row_count)
        return grad_a_rows, early, grads, back

    grad_a_rows, early, grads, (own_one, rest_one, sums_one) = together(
        run, last_group, grad_a, early, grad_heads, qkv[last], lse[last], dqkv, x_all
    )
    dqkv = dqkv + [grads]

    grad_mod = jnp.concatenate([sums_one, sums_two, mlp_sum + fc2_bias * row_sum(grad_out)[None]])
    grad_mod_own = cols_of(grad_mod, tensor_pos)
    for s in range(1, tensor_size):
        owner = lax.rem(tensor_pos - s + tensor_size, tensor_size)
        grad_mod_own = grad_mod_own + shift(cols_of(grad_mod, owner), "tensor", -s)
    grad_mod_own = grad_mod_own.astype(bf16).reshape(6 * local_width)
    late = [
        jnp.concatenate(pair, 1)
        for pair in zip(
            col_grads(hidden_one, [dqkv[last]], core_one, depth),
            col_grads(grad_a_rows, [out[None] for out in heads_out], core_one, depth),
        )
    ]
    grad_vec = jnp.concatenate(
        [row_sum(d[0].astype(f32)) for d in dqkv]
        + [row_sum(d[2].astype(f32)) for d in dqkv]
        + [
            cols_of(row_sum(grad_a_rows.astype(f32)), tensor_pos),
            fc1_sum.reshape(-1),
            cols_of(dm_sum[0], tensor_pos),
        ]
    )

    late = add_low(late[0], xor_step(late[1], "dp", 1))
    total = jnp.concatenate([early, late], 1) if last else late
    side_keep, side_send = side_split(total, depth)

    def side_part(rest_one, side_keep, side_send, grad_mod_own, grad_vec):
        arrived = owners_sum(None, rest_one)[1]
        side = xor_step(side_send, "dp", 2)

        def small(grad_mod_own, grad_vec):
            grad_mod_all = xor_gather(grad_mod_own, True)
            silu_part = dot_nt(grad_mod_all, ada_flat)
            return grad_mod_all, silu_part, xor_sum(grad_vec, True)

        out = together(run, small, grad_mod_own, grad_vec)
        return arrived, far_split(add_low(side_keep, side)), out

    arrived_one, (far_own, far_sends), (grad_mod_all, silu_part, grad_vec) = together(
        run, side_part, rest_one, side_keep, side_send, grad_mod_own, grad_vec
    )

    def far_part(far_own, far_sends, rest_mlp, own_mlp, silu_part, own_one, arrived_one, grad_mod_all):
        arrived_mlp = owners_sum(None, rest_mlp)[1]
        far_arrived = [far_shift(part, s + 1) for s, part in enumerate(far_sends)]

        def small(silu_part, own_one, arrived_one, grad_mod_all):
            grad_hidden_one = add_up(own_one, arrived_one)
            n1, r1 = normed_one[:row_count], rstd_one[:row_count]
            grad_tokens = grad_mid + norm_back(grad_hidden_one * (1.0 + scale_one), n1, r1)
            grad_ada = dot_tn(silu_own, grad_mod_all)
            ada_sum = jnp.sum(grad_mod_all, 0, dtype=f32)
            return grad_tokens.astype(bf16), xor_gather(silu_part, False), grad_ada, ada_sum

        out = together(run, small, silu_part, own_one, arrived_one, grad_mod_all)
        attn_grads = add_up(far_own.astype(f32), far_arrived)
        branch_mlp = add_up(own_mlp, arrived_mlp) + fc2_bias
        block_out = (middle + gate_two * branch_mlp).astype(bf16)
        return block_out, attn_grads, out

    block_out, attn_grads, (grad_tokens, silu_all, grad_ada, ada_sum) = together(
        run, far_part, far_own, far_sends, rest_mlp, own_mlp, silu_part, own_one, arrived_one, grad_mod_all
    )
    grad_ada = grad_ada.reshape(depth, 6, local_width)
    ada_sum = ada_sum.reshape(6, local_width)
    grad_ada_bias = lax.dynamic_slice_in_dim(ada_sum, dp_pos * piece, piece, 1)
    mine = (xor_of(False)[:, None] == xor_of(True)[None, :]).astype(f32)
    silu_rows = sort_xor(jnp.sum(silu_all * mine[:, :, None], 1), False).reshape(1, width)
    grad_silu = silu_rows
    for s in range(1, tensor_size):
        grad_silu = grad_silu + shift(silu_rows, "tensor", s)
    _, silu_back = jax.vjp(jax.nn.silu, cond.astype(f32))
    grad_cond = silu_back(grad_silu)[0]
    grad_qkv = attn_grads[:, : 3 * local_width].reshape(depth, groups, 3, group_width)
    grad_qkv = grad_qkv.transpose(0, 2, 1, 3).reshape(depth, 3, local_width)
    grad_proj = attn_grads[:, 3 * local_width :]

    def own_piece(start, size):
        return lax.dynamic_slice_in_dim(grad_vec, start + dp_pos * size, size, 0)

    grad_qv_bias = jnp.stack([own_piece(0, piece), own_piece(local_width, piece)])
    grad_proj_bias = own_piece(2 * local_width, piece)
    grad_fc1_bias = own_piece(3 * local_width, n_fc1)
    grad_fc2_bias = own_piece(3 * local_width + hidden, piece)

    mlp_grads = mlp_grads.astype(f32)
    return (
        block_out,
        grad_tokens,
        grad_cond,
        grad_qkv,
        grad_qv_bias,
        grad_proj.T,
        grad_proj_bias,
        mlp_grads[:, :hidden],
        grad_fc1_bias,
        mlp_grads[:, hidden:].T,
        grad_fc2_bias,
        grad_ada,
        grad_ada_bias,
    )


def solution(mesh):
    placed = (
        P(("dp", "tensor"), None),
        P("dp", None),
        P(("dp", "tensor"), None),
        P("dp", None, "tensor"),
        P(None, ("tensor", "dp")),
        P("tensor", "dp"),
        P(("tensor", "dp")),
        P("dp", "tensor"),
        P(("tensor", "dp")),
        P("tensor", "dp"),
        P(("tensor", "dp")),
        P("dp", None, "tensor"),
        P(None, ("tensor", "dp")),
    )
    return jax.shard_map(
        shards,
        mesh=mesh,
        in_specs=placed,
        out_specs=(
            P(("dp", "tensor"), None),
            P(("dp", "tensor"), None),
            P("dp", None),
            P("dp", None, "tensor"),
            P(None, ("tensor", "dp")),
            P("tensor", "dp"),
            P(("tensor", "dp")),
            P("dp", "tensor"),
            P(("tensor", "dp")),
            P("tensor", "dp"),
            P(("tensor", "dp")),
            P("dp", None, "tensor"),
            P(None, ("tensor", "dp")),
        ),
        check_vma=False,
    )
```

```python
import math
from functools import partial

import jax
import jax.numpy as jnp
from jax import lax
from jax.experimental import pallas as pl
from jax.experimental.pallas import tpu as pltpu
from jax.sharding import PartitionSpec as P

HEAD_DIM = 64
LEN = 1024
PAIR = 2 * HEAD_DIM

norm_eps = 1e-06
highest = lax.Precision.HIGHEST
f32 = jnp.float32
bf16 = jnp.bfloat16

score_scale = HEAD_DIM ** (-0.5)
log2_scale = score_scale * math.log2(math.e)


MIB = 1024 * 1024


def dot_nn(a, b):
    return lax.dot_general(a, b, (((1,), (0,)), ((), ())), preferred_element_type=f32)


def dot_nt(a, b):
    return lax.dot_general(a, b, (((1,), (1,)), ((), ())), preferred_element_type=f32)


def dot_tn(a, b):
    return lax.dot_general(a, b, (((0,), (0,)), ((), ())), preferred_element_type=f32)


def head_masks():
    lane = lax.broadcasted_iota(jnp.int32, (1, PAIR), 1)
    return [(lane < HEAD_DIM), (lane >= HEAD_DIM)]


def attend_kernel(step_rows, q_ref, k_ref, v_ref, o_ref, lse_ref):
    rows = q_ref.shape[0]
    masks = head_masks()
    keys = k_ref[...]
    values_t = v_ref[...].astype(f32).T.astype(bf16)
    sub = lax.broadcasted_iota(jnp.int32, (PAIR, 1), 0)
    tasks = [(start, head) for start in range(0, rows, step_rows) for head in range(2)]

    def products(task):
        start, head = task
        queries = q_ref[start : start + step_rows, :]
        return dot_nt(keys, jnp.where(masks[head], queries, jnp.zeros_like(queries)))

    ahead = products(tasks[0])
    out_t = []
    for t, (start, head) in enumerate(tasks):
        scores = ahead * log2_scale
        if t + 1 < len(tasks):
            ahead = products(tasks[t + 1])
        peak = jnp.max(scores, 0, keepdims=True)
        terms = jnp.exp2(scores - peak)
        total = jnp.sum(terms, 0, keepdims=True)
        out_t.append(dot_nn(values_t, terms.astype(bf16)) * (1.0 / total))
        lse_ref[0, head : head + 1, start : start + step_rows] = peak + jnp.log2(total)
        if head:
            joined = jnp.where(sub < HEAD_DIM, out_t[0], out_t[1])
            o_ref[start : start + step_rows, :] = joined.T.astype(bf16)
            out_t = []


def attend(qkv, local_width):
    rows = qkv.shape[0]
    pairs = local_width // PAIR
    heads = local_width // HEAD_DIM
    spec = [
        pl.BlockSpec((rows, PAIR), partial(lambda part, i: (0, part * pairs + i), part))
        for part in range(3)
    ]
    return pl.pallas_call(
        partial(attend_kernel, min(512, rows)),
        grid=(pairs,),
        in_specs=spec,
        out_specs=[
            pl.BlockSpec((rows, PAIR), lambda i: (0, i)),
            pl.BlockSpec((1, 2, rows), lambda i: (i, 0, 0)),
        ],
        out_shape=[
            jax.ShapeDtypeStruct((rows, local_width), bf16),
            jax.ShapeDtypeStruct((pairs, 2, rows), f32),
        ],
        compiler_params=pltpu.CompilerParams(vmem_limit_bytes=40 * MIB),
        cost_estimate=pl.CostEstimate(
            flops=4 * heads * rows * rows * 256,
            bytes_accessed=rows * local_width * 8,
            transcendentals=heads * rows * rows,
        ),
        name="attend",
    )(qkv, qkv, qkv)


def attend_back_kernel(step_rows, q_ref, k_ref, v_ref, do_ref, lse_ref, dqkv_ref):
    rows = q_ref.shape[0]
    masks = head_masks()
    keys = k_ref[...]
    values = v_ref[...]
    sub = lax.broadcasted_iota(jnp.int32, (PAIR, 1), 0)
    keys_t = keys.astype(f32).T.astype(bf16)
    d_keys = jnp.zeros((rows, PAIR), f32)
    d_values = jnp.zeros((rows, PAIR), f32)
    tasks = [(start, head) for start in range(0, rows, step_rows) for head in range(2)]

    def products(task):
        start, head = task
        queries = q_ref[start : start + step_rows, :]
        d_out = do_ref[start : start + step_rows, :]
        q_head = jnp.where(masks[head], queries, jnp.zeros_like(queries))
        do_head = jnp.where(masks[head], d_out, jnp.zeros_like(d_out))
        return q_head, do_head, dot_nt(keys, q_head), dot_nt(values, do_head)

    ahead = products(tasks[0])
    dq_t = []
    for t, (start, head) in enumerate(tasks):
        q_head, do_head, scores, d_probs = ahead
        if t + 1 < len(tasks):
            ahead = products(tasks[t + 1])
        lse = lse_ref[0, head : head + 1, start : start + step_rows]
        probs = jnp.exp2(scores * log2_scale - lse)
        weighted = probs * d_probs
        row_dot = jnp.sum(weighted, 0, keepdims=True)
        d_scores = (weighted - probs * row_dot).astype(bf16)
        d_values = d_values + dot_nn(probs.astype(bf16), do_head)
        d_keys = d_keys + dot_nn(d_scores, q_head)
        dq_t.append(dot_nn(keys_t, d_scores))
        if head:
            joined = jnp.where(sub < HEAD_DIM, dq_t[0], dq_t[1])
            dqkv_ref[0, start : start + step_rows, :] = (joined.T * score_scale).astype(bf16)
            dq_t = []
    dqkv_ref[1] = (d_keys * score_scale).astype(bf16)
    dqkv_ref[2] = d_values.astype(bf16)


def attend_back(qkv, grad_heads, lse, local_width):
    rows = qkv.shape[0]
    pairs = local_width // PAIR
    heads = local_width // HEAD_DIM
    spec = [
        pl.BlockSpec((rows, PAIR), partial(lambda part, i: (0, part * pairs + i), part))
        for part in range(3)
    ]
    return pl.pallas_call(
        partial(attend_back_kernel, 256),
        grid=(pairs,),
        in_specs=spec
        + [
            pl.BlockSpec((rows, PAIR), lambda i: (0, i)),
            pl.BlockSpec((1, 2, rows), lambda i: (i, 0, 0)),
        ],
        out_specs=pl.BlockSpec((3, rows, PAIR), lambda i: (0, 0, i)),
        out_shape=jax.ShapeDtypeStruct((3, rows, local_width), bf16),
        compiler_params=pltpu.CompilerParams(vmem_limit_bytes=28 * MIB),
        cost_estimate=pl.CostEstimate(
            flops=10 * heads * rows * rows * 256,
            bytes_accessed=rows * local_width * 14,
            transcendentals=heads * rows * rows,
        ),
        name="attend_back",
    )(qkv, qkv, qkv, grad_heads, lse)


def normalize(values):
    mean = jnp.mean(values, -1, keepdims=True)
    centred = values - mean
    rstd = lax.rsqrt(jnp.mean(centred * centred, -1, keepdims=True) + norm_eps)
    return (centred * rstd, mean, rstd)


def norm_back(grad_n, normed, rstd):
    first = jnp.mean(grad_n, -1, keepdims=True)
    second = jnp.mean(grad_n * normed, -1, keepdims=True)
    return rstd * (grad_n - first - normed * second)


def gelu_both(v):
    c = math.sqrt(2.0 / math.pi)
    sq = v * v
    half = 0.5 + 0.5 * jnp.tanh(v * (c + c * 0.044715 * sq))
    act = v * half
    slope = half + act * (1.0 - half) * (2 * c + 6 * c * 0.044715 * sq)
    return act, slope


def full_spec(shape):
    return pl.BlockSpec(shape, lambda *_: (0,) * len(shape))


def mlp_kernel(
    own_rows, step_rows, h_ref, dm_ref, w1_ref, w2_ref, b1_ref,
    act_ref, dpre_ref, db_ref, own_ref, rest_ref, acc_ref,
):
    j = pl.program_id(0)

    @pl.when(j == 0)
    def _():
        acc_ref[...] = jnp.zeros_like(acc_ref)

    rows = h_ref.shape[0]
    w1, w2, b1 = w1_ref[...], w2_ref[...], b1_ref[...]
    total = jnp.zeros((1, w1.shape[1]), f32)
    for start in range(0, rows, step_rows):
        part = slice(start, start + step_rows)
        pre = dot_nn(h_ref[part, :], w1) + b1
        d_act = dot_nn(dm_ref[part, :], w2)
        act, slope = gelu_both(pre)
        d_pre = d_act * slope
        d_low = d_pre.astype(bf16)
        act_ref[part, :] = act.astype(bf16)
        dpre_ref[part, :] = d_low
        total = total + jnp.sum(d_pre, 0, keepdims=True)
        acc_ref[part, :] += dot_nt(d_low, w1)
    db_ref[...] = total

    @pl.when(j == pl.num_programs(0) - 1)
    def _():
        own_ref[...] = acc_ref[:own_rows, :]
        rest_ref[...] = acc_ref[own_rows:, :].astype(bf16)


def mlp_both(hidden_two, grad_m, mlp_w, bias, own_rows):
    rows, width = hidden_two.shape
    hidden = mlp_w.shape[1] // 2
    block = min(512, hidden)
    steps = hidden // block
    return pl.pallas_call(
        partial(mlp_kernel, own_rows, rows),
        grid=(steps,),
        in_specs=[
            full_spec((rows, width)),
            full_spec((rows, width)),
            pl.BlockSpec((width, block), lambda j: (0, j)),
            pl.BlockSpec((width, block), lambda j: (0, steps + j)),
            pl.BlockSpec((1, block), lambda j: (0, j)),
        ],
        out_specs=[
            pl.BlockSpec((rows, block), lambda j: (0, j)),
            pl.BlockSpec((rows, block), lambda j: (0, j)),
            pl.BlockSpec((1, block), lambda j: (0, j)),
            full_spec((own_rows, width)),
            full_spec((rows - own_rows, width)),
        ],
        out_shape=[
            jax.ShapeDtypeStruct((rows, hidden), bf16),
            jax.ShapeDtypeStruct((rows, hidden), bf16),
            jax.ShapeDtypeStruct((1, hidden), f32),
            jax.ShapeDtypeStruct((own_rows, width), f32),
            jax.ShapeDtypeStruct((rows - own_rows, width), bf16),
        ],
        scratch_shapes=[pltpu.VMEM((rows, width), f32)],
        compiler_params=pltpu.CompilerParams(vmem_limit_bytes=48 * MIB),
        cost_estimate=pl.CostEstimate(
            flops=6 * rows * width * hidden,
            bytes_accessed=4 * rows * hidden + 6 * width * hidden + 8 * rows * width,
            transcendentals=rows * hidden,
        ),
        name="mlp_both",
    )(hidden_two, grad_m, mlp_w, mlp_w, bias)


def transpose_low(value):
    return value.astype(f32).T.astype(bf16)


def mlp_grads_kernel(own_rows, half, h_ref, dm_ref, dpre_ref, act_ref, w2_ref, cot_ref, grad_ref, own_ref, rest_ref, sum_ref, h_t, dm_t, acc_ref):
    j = pl.program_id(0)

    @pl.when(j == 0)
    def _():
        h_t[...] = transpose_low(h_ref[...])
        dm_t[...] = transpose_low(dm_ref[...])
        acc_ref[...] = jnp.zeros_like(acc_ref)

    @pl.when(j < half)
    def _():
        grad_ref[...] = dot_nn(h_t[...], dpre_ref[...]).astype(bf16)

    @pl.when(j >= half)
    def _():
        grad_ref[...] = dot_nn(dm_t[...], act_ref[...]).astype(bf16)
        acc_ref[...] += dot_nt(act_ref[...], w2_ref[...])

    @pl.when(j == 2 * half - 1)
    def _():
        own_ref[...] = acc_ref[:own_rows, :]
        rest_ref[...] = acc_ref[own_rows:, :].astype(bf16)
        sum_ref[...] = jnp.sum(acc_ref[...] * cot_ref[...].astype(f32), 0, keepdims=True)


def mlp_weight_grads(hidden_two, grad_m, grad_pre, activ, mlp_w, cot_all, own_rows):
    rows, width = hidden_two.shape
    hidden = mlp_w.shape[1] // 2
    block = min(512, hidden)
    half = hidden // block
    return pl.pallas_call(
        partial(mlp_grads_kernel, own_rows, half),
        grid=(2 * half,),
        in_specs=[
            full_spec((rows, width)),
            full_spec((rows, width)),
            pl.BlockSpec((rows, block), lambda j: (0, jnp.minimum(j, half - 1))),
            pl.BlockSpec((rows, block), lambda j: (0, jnp.maximum(j - half, 0))),
            pl.BlockSpec((width, block), lambda j: (0, half + jnp.maximum(j - half, 0))),
            full_spec((rows, width)),
        ],
        out_specs=[
            pl.BlockSpec((width, block), lambda j: (0, j)),
            full_spec((own_rows, width)),
            full_spec((rows - own_rows, width)),
            full_spec((1, width)),
        ],
        out_shape=[
            jax.ShapeDtypeStruct((width, 2 * hidden), bf16),
            jax.ShapeDtypeStruct((own_rows, width), f32),
            jax.ShapeDtypeStruct((rows - own_rows, width), bf16),
            jax.ShapeDtypeStruct((1, width), f32),
        ],
        scratch_shapes=[
            pltpu.VMEM((width, rows), bf16),
            pltpu.VMEM((width, rows), bf16),
            pltpu.VMEM((rows, width), f32),
        ],
        compiler_params=pltpu.CompilerParams(vmem_limit_bytes=48 * MIB),
        cost_estimate=pl.CostEstimate(
            flops=6 * rows * width * hidden,
            bytes_accessed=4 * rows * hidden + 6 * width * hidden + 8 * rows * width,
            transcendentals=0,
        ),
        name="mlp_weight_grads",
    )(hidden_two, grad_m, grad_pre, activ, mlp_w, cot_all)


def middle_kernel(own_steps, pieces, *refs):
    heads = [ref[...] for ref in refs[:pieces]]
    w_ref, x_ref, cot_ref, mod_ref = refs[pieces : pieces + 4]
    h_ref, dm_ref, sum_ref, a_ref, x1_ref, mean_ref, rstd_ref = refs[pieces + 4 :]
    i = pl.program_id(0)
    branch = dot_nt(jnp.concatenate(heads, 1), w_ref[...]) + mod_ref[6:7, :]
    middle = x_ref[...].astype(f32) + mod_ref[2:3, :] * branch
    normed, mean, rstd = normalize(middle)
    h_ref[...] = (normed * (1.0 + mod_ref[4:5, :]) + mod_ref[3:4, :]).astype(bf16)
    low = (mod_ref[5:6, :] * cot_ref[...].astype(f32)).astype(bf16)
    dm_ref[...] = low
    total = jnp.sum(low.astype(f32), 0, keepdims=True)

    @pl.when(i == 0)
    def _():
        sum_ref[...] = total

    @pl.when(i > 0)
    def _():
        sum_ref[...] += total

    @pl.when(i < own_steps)
    def _():
        a_ref[...] = branch
        x1_ref[...] = middle
        mean_ref[...] = mean
        rstd_ref[...] = rstd


def middle_part(heads, weight, x_all, cot_all, modul, own_rows):
    rows, width = x_all.shape
    block = min(256, own_rows)
    steps, own_steps = rows // block, own_rows // block
    specs, arrays = [], []
    for s, parts in enumerate(heads):
        for part in parts:
            specs.append(
                pl.BlockSpec(
                    (block, part.shape[1]),
                    partial(lambda back, i: (lax.rem(i - back + steps, steps), 0), s * own_steps),
                )
            )
            arrays.append(part)
    row_spec = pl.BlockSpec((block, width), lambda i: (i, 0))
    own_spec = pl.BlockSpec((block, width), lambda i: (jnp.minimum(i, own_steps - 1), 0))
    one_spec = pl.BlockSpec((block, 1), lambda i: (jnp.minimum(i, own_steps - 1), 0))
    return pl.pallas_call(
        partial(middle_kernel, own_steps, len(arrays)),
        grid=(steps,),
        in_specs=specs
        + [full_spec((width, width)), row_spec, row_spec, full_spec(modul.shape)],
        out_specs=[row_spec, row_spec, full_spec((1, width)), own_spec, own_spec, one_spec, one_spec],
        out_shape=[
            jax.ShapeDtypeStruct((rows, width), bf16),
            jax.ShapeDtypeStruct((rows, width), bf16),
            jax.ShapeDtypeStruct((1, width), f32),
            jax.ShapeDtypeStruct((own_rows, width), f32),
            jax.ShapeDtypeStruct((own_rows, width), f32),
            jax.ShapeDtypeStruct((own_rows, 1), f32),
            jax.ShapeDtypeStruct((own_rows, 1), f32),
        ],
        compiler_params=pltpu.CompilerParams(vmem_limit_bytes=40 * MIB),
        cost_estimate=pl.CostEstimate(
            flops=2 * rows * width * width,
            bytes_accessed=12 * rows * width + 8 * own_rows * width,
            transcendentals=rows,
        ),
        name="middle_part",
    )(*arrays, weight, x_all, cot_all, modul)


def middle_back_kernel(others, pieces, own_ref, *refs):
    arrived = refs[:others]
    cot_ref, x1_ref, a_ref, mean_ref, rstd_ref, mod_ref, w_ref = refs[others : others + 7]
    mid_ref, da_ref, sums_ref = refs[others + 7 : others + 10]
    head_refs = refs[others + 10 :]
    grad_h = own_ref[...]
    for ref in arrived:
        grad_h = grad_h + ref[...].astype(f32)
    normed = (x1_ref[...] - mean_ref[...]) * rstd_ref[...]
    grad_mid = cot_ref[...].astype(f32) + norm_back(
        grad_h * (1.0 + mod_ref[4:5, :]), normed, rstd_ref[...]
    )
    grad_a = (mod_ref[2:3, :] * grad_mid).astype(bf16)
    mid_ref[...] = grad_mid
    da_ref[...] = grad_a
    sums = jnp.concatenate(
        [
            jnp.sum(grad_mid * a_ref[...], 0, keepdims=True),
            jnp.sum(grad_h, 0, keepdims=True),
            jnp.sum(grad_h * normed, 0, keepdims=True),
        ]
    )
    i = pl.program_id(0)

    @pl.when(i == 0)
    def _():
        sums_ref[...] = sums

    @pl.when(i > 0)
    def _():
        sums_ref[...] += sums

    grad_heads = dot_nn(grad_a, w_ref[...]).astype(bf16)
    columns = head_refs[0].shape[1]
    for p in range(pieces):
        head_refs[p][...] = grad_heads[:, p * columns : (p + 1) * columns]


def middle_back(own, arrived, cot, x1, branch, mean, rstd, modul, weight, columns):
    rows, width = own.shape
    block = min(256, rows)
    pieces = width // columns
    row_spec = pl.BlockSpec((block, width), lambda i: (i, 0))
    one_spec = pl.BlockSpec((block, 1), lambda i: (i, 0))
    return pl.pallas_call(
        partial(middle_back_kernel, len(arrived), pieces),
        grid=(rows // block,),
        in_specs=[row_spec] * (len(arrived) + 4)
        + [one_spec, one_spec, full_spec(modul.shape), full_spec((width, width))],
        out_specs=[row_spec, row_spec, full_spec((3, width))]
        + [pl.BlockSpec((block, columns), lambda i: (i, 0))] * pieces,
        out_shape=[
            jax.ShapeDtypeStruct((rows, width), f32),
            jax.ShapeDtypeStruct((rows, width), bf16),
            jax.ShapeDtypeStruct((3, width), f32),
        ]
        + [jax.ShapeDtypeStruct((rows, columns), bf16)] * pieces,
        compiler_params=pltpu.CompilerParams(vmem_limit_bytes=40 * MIB),
        cost_estimate=pl.CostEstimate(
            flops=2 * rows * width * width, bytes_accessed=28 * rows * width, transcendentals=0
        ),
        name="middle_back",
    )(own, *arrived, cot, x1, branch, mean, rstd, modul, weight)


def col_grads_kernel(count, depth, arrays, core_ref, left_ref, *refs):
    keep_ref, send_ref = refs[arrays:]
    left_t = transpose_low(left_ref[...])
    core = core_ref[0]
    at = 0
    for ref in refs[:arrays]:
        for p in range(ref.shape[0]):
            columns = slice(at, at + ref.shape[2])
            result = dot_nn(left_t, ref[p])
            for i in range(count // 2):
                low = result[2 * i * depth : (2 * i + 1) * depth]
                high = result[(2 * i + 1) * depth : (2 * i + 2) * depth]
                rows = slice(i * depth, (i + 1) * depth)
                keep_ref[rows, columns] = jnp.where(core == 0, low, high).astype(bf16)
                send_ref[rows, columns] = jnp.where(core == 0, high, low).astype(bf16)
            at += ref.shape[2]


def col_grads(left, rights, core, depth):
    rows, width = left.shape
    columns = sum(right.shape[0] * right.shape[2] for right in rights)
    out = jax.ShapeDtypeStruct((width // 2, columns), bf16)
    vmem = pl.BlockSpec(memory_space=pltpu.VMEM)
    return pl.pallas_call(
        partial(col_grads_kernel, width // depth, depth, len(rights)),
        in_specs=[pl.BlockSpec(memory_space=pltpu.SMEM)] + [vmem] * (1 + len(rights)),
        out_specs=[vmem, vmem],
        out_shape=[out, out],
        compiler_params=pltpu.CompilerParams(vmem_limit_bytes=40 * MIB),
        cost_estimate=pl.CostEstimate(
            flops=2 * rows * width * columns,
            bytes_accessed=2 * rows * width + 4 * rows * columns,
            transcendentals=0,
        ),
        name="col_grads",
    )(core, left, *rights)


def hidden_back_kernel(own_steps, first, x_ref, w_ref, *refs):
    own_ref, rest_ref, sums_ref = refs[-3:]
    pieces = [ref[p] for ref in refs[:-3] for p in range(3)]
    total = dot_nt(jnp.concatenate(pieces, 1), w_ref[:, first:])
    normed, _, _ = normalize(x_ref[...].astype(f32))
    sums = jnp.concatenate(
        [jnp.sum(total, 0, keepdims=True), jnp.sum(total * normed, 0, keepdims=True)]
    )
    i = pl.program_id(0)

    @pl.when(i == 0)
    def _():
        sums_ref[...] = sums

    @pl.when(i > 0)
    def _():
        sums_ref[...] += sums

    @pl.when(i < own_steps)
    def _():
        own_ref[...] = total

    @pl.when(i >= own_steps)
    def _():
        rest_ref[...] = total.astype(bf16)


def hidden_back(x_all, grads, weight, first, own_rows):
    rows, width = x_all.shape
    columns = grads[0].shape[2]
    block = min(256, own_rows)
    own_steps = own_rows // block
    return pl.pallas_call(
        partial(hidden_back_kernel, own_steps, first),
        grid=(rows // block,),
        in_specs=[pl.BlockSpec((block, width), lambda i: (i, 0)), full_spec(weight.shape)]
        + [pl.BlockSpec((3, block, columns), lambda i: (0, i, 0))] * len(grads),
        out_specs=[
            pl.BlockSpec((block, width), lambda i: (jnp.minimum(i, own_steps - 1), 0)),
            pl.BlockSpec((block, width), lambda i: (jnp.maximum(i - own_steps, 0), 0)),
            full_spec((2, width)),
        ],
        out_shape=[
            jax.ShapeDtypeStruct((own_rows, width), f32),
            jax.ShapeDtypeStruct((rows - own_rows, width), bf16),
            jax.ShapeDtypeStruct((2, width), f32),
        ],
        compiler_params=pltpu.CompilerParams(vmem_limit_bytes=40 * MIB),
        cost_estimate=pl.CostEstimate(
            flops=6 * rows * width * columns * len(grads),
            bytes_accessed=4 * rows * width + 12 * rows * columns * len(grads),
            transcendentals=0,
        ),
        name="hidden_back",
    )(x_all, weight, *grads)


def shift(x, axis, step):
    size = lax.axis_size(axis)
    return lax.ppermute(x, axis, [(i, (i + step) % size) for i in range(size)])


def xor_step(x, axis, bit):
    size = lax.axis_size(axis)
    return lax.ppermute(x, axis, [(i, i ^ bit) for i in range(size)])


def bits_of(side_last):
    size = lax.axis_size("dp")
    bits = [1 << k for k in range(size.bit_length() - 1)]
    return bits[:1] + bits[2:] + bits[1:2] if side_last else bits


def xor_of(side_last):
    bits = bits_of(side_last)
    place = jnp.arange(1 << len(bits), dtype=jnp.int32)
    return sum(((place >> k) & 1) * bit for k, bit in enumerate(bits))


def xor_gather(x, side_last):
    return widen(x[None], bits_of(side_last))


def widen(out, bits):
    for bit in bits:
        out = jnp.concatenate([out, xor_step(out, "dp", bit)], 0)
    return out


def xor_scatter_sum(x, side_last):
    half = x.shape[0] // 2
    for bit in reversed(bits_of(side_last)):
        x = x[:half] + xor_step(x[half:], "dp", bit)
        half //= 2
    return x[0]


def xor_sum(x, side_last):
    for bit in bits_of(side_last):
        x = x + xor_step(x, "dp", bit)
    return x


def sort_xor(x, side_last):
    size = lax.axis_size("dp")
    me = lax.axis_index("dp")
    order = jnp.arange(size, dtype=jnp.int32)
    pick = ((order[:, None] ^ me) == xor_of(side_last)[None, :]).astype(f32)
    flat = x.reshape(size, -1).astype(f32)
    return jnp.dot(pick, flat, precision=highest).reshape(x.shape)


def rel_gather(x, axis):
    return [x] + [shift(x, axis, s) for s in range(1, lax.axis_size(axis))]


def sort_rel(parts, axis):
    size = lax.axis_size(axis)
    me = lax.axis_index(axis)
    out = []
    for target in range(size):
        value = jnp.zeros_like(parts[0])
        for s in range(size):
            value = jnp.where(lax.rem(me - s + size, size) == target, parts[s], value)
        out.append(value)
    return out


def together(run, work, *args):
    shapes = jax.eval_shape(work, *args)
    empty = lambda *_: jax.tree.map(lambda v: jnp.zeros(v.shape, v.dtype), shapes)
    return lax.cond(run, work, empty, *args)


def dp_place():
    size, me = lax.axis_size("dp"), lax.axis_index("dp")
    return size // 4, me // 4, lax.rem(me // 2, 2), lax.rem(me, 2)


def after(value, *others):
    return lax.optimization_barrier((value,) + others)[0]


def far_shift(x, step):
    size = lax.axis_size("dp")
    return lax.ppermute(x, "dp", [(i, (i + 4 * step) % size) for i in range(size)])


def add_low(keep, arrived):
    return (keep.astype(f32) + arrived.astype(f32)).astype(bf16)


def side_split(total, depth):
    far_size, _, side, _ = dp_place()
    total = total.reshape(far_size, 2, depth, total.shape[1])
    keep = lax.dynamic_index_in_dim(total, side, 1, keepdims=False)
    return keep, lax.dynamic_index_in_dim(total, 1 - side, 1, keepdims=False)


def far_split(total):
    far_size, far, _, _ = dp_place()
    rows = [
        lax.dynamic_index_in_dim(total, lax.rem(far + s, far_size), 0, keepdims=False)
        for s in range(far_size)
    ]
    return rows[0], rows[1:]


def shards(
    tokens, cond, cotangent, w_qkv, b_qv, w_proj, b_proj, w_fc1, b_fc1, w_fc2, b_fc2, w_ada, b_ada
):
    tensor_size = lax.axis_size("tensor")
    dp_size = lax.axis_size("dp")
    tensor_pos = lax.axis_index("tensor")
    dp_pos = lax.axis_index("dp")
    row_count, width = tokens.shape
    group_rows = row_count * tensor_size
    depth = w_qkv.shape[0]
    local_width = w_qkv.shape[2]
    hidden = w_fc1.shape[1]
    pairs = local_width // PAIR
    groups = 2 if pairs % 2 == 0 else 1
    group_width = local_width // groups
    assert cond.shape[0] == 1 and group_rows == LEN

    def row_sum(v):
        return jnp.sum(v, 0, dtype=f32)

    def cols_of(values, owner):
        return lax.dynamic_slice_in_dim(values, owner * local_width, local_width, values.ndim - 1)

    run = dp_pos >= 0
    qkv_parts = [
        w_qkv[:, :, g * group_width : (g + 1) * group_width].reshape(depth, 3 * group_width)
        for g in range(groups)
    ]
    attn_w = lax.all_gather(jnp.concatenate([w_proj.T] + qkv_parts, 1), "dp", axis=0, tiled=True)
    mlp_w = lax.all_gather(jnp.concatenate([w_fc1, w_fc2.T], 1), "dp", axis=0, tiled=True)
    x_all = jnp.concatenate(rel_gather(tokens, "tensor"), 0)
    core_one = lax.rem(dp_pos, 2).astype(jnp.int32).reshape(1)

    vectors = jnp.concatenate([b_qv.reshape(-1), b_fc1])
    packed = xor_gather(jnp.concatenate([cond.reshape(-1), vectors]), True)
    cond_all = packed[:, :width]
    own_vec = sort_xor(packed[:, width:], True)
    piece = b_proj.shape[0]
    n_fc1 = b_fc1.shape[0]
    qv_bias = own_vec[:, : 2 * piece].reshape(dp_size, 2, piece).transpose(1, 0, 2)
    qv_bias = qv_bias.reshape(2, local_width)
    fc1_bias = own_vec[:, 2 * piece :].reshape(1, hidden)

    silu_all = jax.nn.silu(cond_all.astype(f32)).astype(bf16)
    silu_own = lax.dynamic_slice(silu_all, (0, dp_pos * depth), (dp_size, depth))
    ada_flat = w_ada.reshape(depth, 6 * local_width)
    biases = jnp.concatenate([b_ada, b_proj[None], b_fc2[None]]).astype(f32)
    lane = lax.broadcasted_iota(jnp.int32, (1, local_width), 1)
    biases = jnp.where(lane // piece == dp_pos, jnp.tile(biases, (1, dp_size)), 0.0)
    mod_part = jnp.pad(dot_nn(silu_own, ada_flat), ((0, 0), (0, 2 * local_width)))
    mod_part = mod_part + biases.reshape(1, 8 * local_width)
    mod_half = xor_scatter_sum(mod_part, True).reshape(8, local_width)
    modul = jnp.concatenate(sort_rel(rel_gather(mod_half, "tensor"), "tensor"), 1)
    shift_one, scale_one, gate_one, shift_two, scale_two, gate_two, proj_bias, fc2_bias = [
        modul[k : k + 1] for k in range(8)
    ]

    def first_rows(cotangent, x_all, shift_one, scale_one):
        moved = rel_gather(cotangent, "tensor")[1:]
        normed, _, rstd = normalize(x_all.astype(f32))
        return moved, (normed * (1.0 + scale_one) + shift_one).astype(bf16)

    cot_parts, hidden_one = together(run, first_rows, cotangent, x_all, shift_one, scale_one)
    cot_all = jnp.concatenate([cotangent] + cot_parts, 0)
    normed_one, _, rstd_one = normalize(tokens.astype(f32))

    def attend_group(g, moving, hidden_one, attn_w, qv_bias):
        moved = rel_gather(moving, "tensor")[1:]
        cols = slice(g * group_width, (g + 1) * group_width)
        bias = jnp.concatenate([qv_bias[0, cols], jnp.zeros((group_width,), f32), qv_bias[1, cols]])
        at = local_width + 3 * group_width * g
        weight = attn_w[:, at : at + 3 * group_width]
        qkv = (dot_nn(hidden_one, weight) + bias).astype(bf16)
        return moved, qkv, attend(qkv, group_width)

    qkv, heads_out, lse, moved = [], [], [], []
    for g in range(groups):
        moving = heads_out[g - 1] if g else attn_w[:, :local_width]
        parts, qkv_g, (out, log_total) = together(
            run, partial(attend_group, g), moving, hidden_one, attn_w, qv_bias
        )
        qkv.append(qkv_g)
        heads_out.append(out)
        lse.append(log_total)
        moved.append(parts)
    moved.append(rel_gather(heads_out[-1], "tensor")[1:])
    proj_w = jnp.concatenate([attn_w[:, :local_width]] + moved[0], 1)
    heads_other = moved[1:]
    heads_rel = [heads_out] + [[v[s - 1] for v in heads_other] for s in range(1, tensor_size)]
    hidden_two, grad_m, dm_sum, branch_attn, middle, mean_two, rstd_two = middle_part(
        heads_rel, proj_w, x_all, cot_all, modul, row_count
    )

    activ, grad_pre, fc1_sum, own_two, rest_two = mlp_both(
        hidden_two, grad_m, mlp_w, fc1_bias, row_count
    )

    def owners_sum(own, rest):
        arrived = [
            shift(rest[(s - 1) * row_count : s * row_count], "tensor", -s)
            for s in range(1, tensor_size)
        ]
        return own, arrived

    def add_up(own, arrived):
        for part in arrived:
            own = own + part.astype(f32)
        return own

    def weight_part(rest_two, *args):
        arrived = owners_sum(None, rest_two)[1]
        return arrived, mlp_weight_grads(*args, row_count)

    arrived_two, (mlp_grads, own_mlp, rest_mlp, mlp_sum) = together(
        run, weight_part, rest_two, hidden_two, grad_m, grad_pre, activ, mlp_w, cot_all
    )
    mlp_grads = lax.psum_scatter(mlp_grads, "dp", scatter_dimension=0, tiled=True)

    grad_out = cotangent.astype(f32)
    grad_mid, grad_a, sums_two, *grad_pieces = middle_back(
        own_two, arrived_two, cotangent, middle, branch_attn, mean_two, rstd_two, modul, proj_w, group_width
    )

    def heads_of(pieces, g):
        parts = [pieces[g]]
        for j in range(1, tensor_size):
            s = tensor_size - j
            parts.append(shift(pieces[s * groups + g], "tensor", -s))
        return jnp.concatenate(parts, 0)

    last = groups - 1
    grad_heads = heads_of(grad_pieces, 0)
    dqkv, early = [], []
    if last:

        def first_group(pieces, heads, qkv_g, lse_g, left):
            moved = heads_of(pieces, 1)
            grads = attend_back(qkv_g, heads, lse_g, group_width)
            return moved, grads, col_grads(left, [grads], core_one, depth)

        grad_heads, grads, early = together(
            run, first_group, grad_pieces, grad_heads, qkv[0], lse[0], hidden_one
        )
        dqkv.append(grads)

    def last_group(grad_a, early, heads, qkv_g, lse_g, before, x_all):
        grad_a_rows = jnp.concatenate(rel_gather(grad_a, "tensor"), 0)
        if early:
            early = add_low(early[0], xor_step(early[1], "dp", 1))
        grads = attend_back(qkv_g, heads, lse_g, group_width)
        back = hidden_back(x_all, before + [grads], attn_w, local_width, row_count)
        return grad_a_rows, early, grads, back

    grad_a_rows, early, grads, (own_one, rest_one, sums_one) = together(
        run, last_group, grad_a, early, grad_heads, qkv[last], lse[last], dqkv, x_all
    )
    dqkv = dqkv + [grads]

    grad_mod = jnp.concatenate([sums_one, sums_two, mlp_sum + fc2_bias * row_sum(grad_out)[None]])
    grad_mod_own = cols_of(grad_mod, tensor_pos)
    for s in range(1, tensor_size):
        owner = lax.rem(tensor_pos - s + tensor_size, tensor_size)
        grad_mod_own = grad_mod_own + shift(cols_of(grad_mod, owner), "tensor", -s)
    grad_mod_own = grad_mod_own.astype(bf16).reshape(6 * local_width)
    late = [
        jnp.concatenate(pair, 1)
        for pair in zip(
            col_grads(hidden_one, [dqkv[last]], core_one, depth),
            col_grads(grad_a_rows, [out[None] for out in heads_out], core_one, depth),
        )
    ]
    grad_vec = jnp.concatenate(
        [row_sum(d[0].astype(f32)) for d in dqkv]
        + [row_sum(d[2].astype(f32)) for d in dqkv]
        + [
            cols_of(row_sum(grad_a_rows.astype(f32)), tensor_pos),
            fc1_sum.reshape(-1),
            cols_of(dm_sum[0], tensor_pos),
        ]
    )

    late = add_low(late[0], xor_step(late[1], "dp", 1))
    total = jnp.concatenate([early, late], 1) if last else late
    side_keep, side_send = side_split(total, depth)

    def side_part(rest_one, side_keep, side_send, grad_mod_own, grad_vec):
        arrived = owners_sum(None, rest_one)[1]
        side = xor_step(side_send, "dp", 2)

        def small(grad_mod_own, grad_vec):
            grad_mod_all = xor_gather(grad_mod_own, True)
            silu_part = dot_nt(grad_mod_all, ada_flat)
            return grad_mod_all, silu_part, xor_sum(grad_vec, True)

        out = together(run, small, grad_mod_own, grad_vec)
        return arrived, far_split(add_low(side_keep, side)), out

    arrived_one, (far_own, far_sends), (grad_mod_all, silu_part, grad_vec) = together(
        run, side_part, rest_one, side_keep, side_send, grad_mod_own, grad_vec
    )

    def own_piece(values, start, size):
        return lax.dynamic_slice_in_dim(values, start + dp_pos * size, size, 0)

    def far_part(far_own, far_sends, rest_mlp, own_mlp, *args):
        arrived_mlp = owners_sum(None, rest_mlp)[1]
        far_arrived = [far_shift(part, s + 1) for s, part in enumerate(far_sends)]

        def small(silu_part, *values):
            near = widen(silu_part[None], bits_of(False)[:2])
            near, own_one, arrived_one, grad_mod_all, grad_vec, mlp_grads = lax.optimization_barrier(
                (near,) + values
            )
            silu_all = widen(near, bits_of(False)[2:])
            grad_hidden_one = add_up(own_one, arrived_one)
            grad_tokens = grad_mid + norm_back(
                grad_hidden_one * (1.0 + scale_one), normed_one, rstd_one
            )
            grad_ada = dot_tn(silu_own, grad_mod_all).reshape(depth, 6, local_width)
            ada_sum = jnp.sum(grad_mod_all, 0, dtype=f32).reshape(6, local_width)
            vectors = (
                lax.dynamic_slice_in_dim(ada_sum, dp_pos * piece, piece, 1),
                jnp.stack([own_piece(grad_vec, 0, piece), own_piece(grad_vec, local_width, piece)]),
                own_piece(grad_vec, 2 * local_width, piece),
                own_piece(grad_vec, 3 * local_width, n_fc1),
                own_piece(grad_vec, 3 * local_width + hidden, piece),
            )
            mlp_grads = mlp_grads.astype(f32)
            mlp_grads = (mlp_grads[:, :hidden], mlp_grads[:, hidden:].T)
            mine = (xor_of(False)[:, None] == xor_of(True)[None, :]).astype(f32)
            silu_rows = sort_xor(jnp.sum(silu_all * mine[:, :, None], 1), False)
            return grad_tokens.astype(bf16), silu_rows.reshape(1, width), grad_ada, vectors, mlp_grads

        out = together(run, small, *args)
        attn_grads = add_up(far_own.astype(f32), far_arrived)
        branch_mlp = add_up(own_mlp, arrived_mlp) + fc2_bias
        block_out = (middle + gate_two * branch_mlp).astype(bf16)
        return block_out, attn_grads, out

    block_out, attn_grads, out = together(
        run,
        far_part,
        far_own,
        far_sends,
        rest_mlp,
        own_mlp,
        silu_part,
        own_one,
        arrived_one,
        grad_mod_all,
        grad_vec,
        mlp_grads,
    )
    grad_tokens, silu_rows, grad_ada, vectors, (grad_fc1, grad_fc2) = out
    grad_ada_bias, grad_qv_bias, grad_proj_bias, grad_fc1_bias, grad_fc2_bias = vectors
    grad_silu = silu_rows
    for s in range(1, tensor_size):
        grad_silu = grad_silu + shift(silu_rows, "tensor", s)
    _, silu_back = jax.vjp(jax.nn.silu, cond.astype(f32))
    grad_cond = silu_back(grad_silu)[0]
    grad_qkv = attn_grads[:, : 3 * local_width].reshape(depth, groups, 3, group_width)
    grad_qkv = grad_qkv.transpose(0, 2, 1, 3).reshape(depth, 3, local_width)
    return (
        block_out,
        grad_tokens,
        grad_cond,
        grad_qkv,
        grad_qv_bias,
        attn_grads[:, 3 * local_width :].T,
        grad_proj_bias,
        grad_fc1,
        grad_fc1_bias,
        grad_fc2,
        grad_fc2_bias,
        grad_ada,
        grad_ada_bias,
    )


def solution(mesh):
    placed = (
        P(("dp", "tensor"), None),
        P("dp", None),
        P(("dp", "tensor"), None),
        P("dp", None, "tensor"),
        P(None, ("tensor", "dp")),
        P("tensor", "dp"),
        P(("tensor", "dp")),
        P("dp", "tensor"),
        P(("tensor", "dp")),
        P("tensor", "dp"),
        P(("tensor", "dp")),
        P("dp", None, "tensor"),
        P(None, ("tensor", "dp")),
    )
    return jax.shard_map(
        shards,
        mesh=mesh,
        in_specs=placed,
        out_specs=(
            P(("dp", "tensor"), None),
            P(("dp", "tensor"), None),
            P("dp", None),
            P("dp", None, "tensor"),
            P(None, ("tensor", "dp")),
            P("tensor", "dp"),
            P(("tensor", "dp")),
            P("dp", "tensor"),
            P(("tensor", "dp")),
            P("tensor", "dp"),
            P(("tensor", "dp")),
            P("dp", None, "tensor"),
            P(None, ("tensor", "dp")),
        ),
        check_vma=False,
    )
```

```python
import math
from functools import partial

import jax
import jax.numpy as jnp
from jax import lax
from jax.experimental import pallas as pl
from jax.experimental.pallas import tpu as pltpu
from jax.sharding import PartitionSpec as P

HEAD_DIM = 64
LEN = 1024
PAIR = 2 * HEAD_DIM

norm_eps = 1e-06
highest = lax.Precision.HIGHEST
f32 = jnp.float32
bf16 = jnp.bfloat16

score_scale = HEAD_DIM ** (-0.5)
log2_scale = score_scale * math.log2(math.e)


MIB = 1024 * 1024


def dot_nn(a, b):
    return lax.dot_general(a, b, (((1,), (0,)), ((), ())), preferred_element_type=f32)


def dot_nt(a, b):
    return lax.dot_general(a, b, (((1,), (1,)), ((), ())), preferred_element_type=f32)


def dot_tn(a, b):
    return lax.dot_general(a, b, (((0,), (0,)), ((), ())), preferred_element_type=f32)


def head_masks():
    lane = lax.broadcasted_iota(jnp.int32, (1, PAIR), 1)
    return [(lane < HEAD_DIM), (lane >= HEAD_DIM)]


def attend_kernel(step_rows, q_ref, k_ref, v_ref, o_ref, lse_ref):
    rows = q_ref.shape[0]
    masks = head_masks()
    keys = k_ref[...]
    values_t = v_ref[...].astype(f32).T.astype(bf16)
    sub = lax.broadcasted_iota(jnp.int32, (PAIR, 1), 0)
    tasks = [(start, head) for start in range(0, rows, step_rows) for head in range(2)]

    def products(task):
        start, head = task
        queries = q_ref[start : start + step_rows, :]
        return dot_nt(keys, jnp.where(masks[head], queries, jnp.zeros_like(queries)))

    ahead = products(tasks[0])
    out_t = []
    for t, (start, head) in enumerate(tasks):
        scores = ahead * log2_scale
        if t + 1 < len(tasks):
            ahead = products(tasks[t + 1])
        peak = jnp.max(scores, 0, keepdims=True)
        terms = jnp.exp2(scores - peak)
        total = jnp.sum(terms, 0, keepdims=True)
        out_t.append(dot_nn(values_t, terms.astype(bf16)) * (1.0 / total))
        lse_ref[0, head : head + 1, start : start + step_rows] = peak + jnp.log2(total)
        if head:
            joined = jnp.where(sub < HEAD_DIM, out_t[0], out_t[1])
            o_ref[start : start + step_rows, :] = joined.T.astype(bf16)
            out_t = []


def attend(qkv, local_width):
    rows = qkv.shape[0]
    pairs = local_width // PAIR
    heads = local_width // HEAD_DIM
    spec = [
        pl.BlockSpec((rows, PAIR), partial(lambda part, i: (0, part * pairs + i), part))
        for part in range(3)
    ]
    return pl.pallas_call(
        partial(attend_kernel, min(512, rows)),
        grid=(pairs,),
        in_specs=spec,
        out_specs=[
            pl.BlockSpec((rows, PAIR), lambda i: (0, i)),
            pl.BlockSpec((1, 2, rows), lambda i: (i, 0, 0)),
        ],
        out_shape=[
            jax.ShapeDtypeStruct((rows, local_width), bf16),
            jax.ShapeDtypeStruct((pairs, 2, rows), f32),
        ],
        compiler_params=pltpu.CompilerParams(vmem_limit_bytes=40 * MIB),
        cost_estimate=pl.CostEstimate(
            flops=4 * heads * rows * rows * 256,
            bytes_accessed=rows * local_width * 8,
            transcendentals=heads * rows * rows,
        ),
        name="attend",
    )(qkv, qkv, qkv)


def attend_back_kernel(step_rows, q_ref, k_ref, v_ref, do_ref, lse_ref, dqkv_ref):
    rows = q_ref.shape[0]
    masks = head_masks()
    keys = k_ref[...]
    values = v_ref[...]
    sub = lax.broadcasted_iota(jnp.int32, (PAIR, 1), 0)
    keys_t = keys.astype(f32).T.astype(bf16)
    d_keys = jnp.zeros((rows, PAIR), f32)
    d_values = jnp.zeros((rows, PAIR), f32)
    tasks = [(start, head) for start in range(0, rows, step_rows) for head in range(2)]

    def products(task):
        start, head = task
        queries = q_ref[start : start + step_rows, :]
        d_out = do_ref[start : start + step_rows, :]
        q_head = jnp.where(masks[head], queries, jnp.zeros_like(queries))
        do_head = jnp.where(masks[head], d_out, jnp.zeros_like(d_out))
        return q_head, do_head, dot_nt(keys, q_head), dot_nt(values, do_head)

    ahead = products(tasks[0])
    dq_t = []
    for t, (start, head) in enumerate(tasks):
        q_head, do_head, scores, d_probs = ahead
        if t + 1 < len(tasks):
            ahead = products(tasks[t + 1])
        lse = lse_ref[0, head : head + 1, start : start + step_rows]
        probs = jnp.exp2(scores * log2_scale - lse)
        weighted = probs * d_probs
        row_dot = jnp.sum(weighted, 0, keepdims=True)
        d_scores = (weighted - probs * row_dot).astype(bf16)
        d_values = d_values + dot_nn(probs.astype(bf16), do_head)
        d_keys = d_keys + dot_nn(d_scores, q_head)
        dq_t.append(dot_nn(keys_t, d_scores))
        if head:
            joined = jnp.where(sub < HEAD_DIM, dq_t[0], dq_t[1])
            dqkv_ref[0, start : start + step_rows, :] = (joined.T * score_scale).astype(bf16)
            dq_t = []
    dqkv_ref[1] = (d_keys * score_scale).astype(bf16)
    dqkv_ref[2] = d_values.astype(bf16)


def attend_back(qkv, grad_heads, lse, local_width):
    rows = qkv.shape[0]
    pairs = local_width // PAIR
    heads = local_width // HEAD_DIM
    spec = [
        pl.BlockSpec((rows, PAIR), partial(lambda part, i: (0, part * pairs + i), part))
        for part in range(3)
    ]
    return pl.pallas_call(
        partial(attend_back_kernel, 256),
        grid=(pairs,),
        in_specs=spec
        + [
            pl.BlockSpec((rows, PAIR), lambda i: (0, i)),
            pl.BlockSpec((1, 2, rows), lambda i: (i, 0, 0)),
        ],
        out_specs=pl.BlockSpec((3, rows, PAIR), lambda i: (0, 0, i)),
        out_shape=jax.ShapeDtypeStruct((3, rows, local_width), bf16),
        compiler_params=pltpu.CompilerParams(vmem_limit_bytes=28 * MIB),
        cost_estimate=pl.CostEstimate(
            flops=10 * heads * rows * rows * 256,
            bytes_accessed=rows * local_width * 14,
            transcendentals=heads * rows * rows,
        ),
        name="attend_back",
    )(qkv, qkv, qkv, grad_heads, lse)


def normalize(values):
    mean = jnp.mean(values, -1, keepdims=True)
    centred = values - mean
    rstd = lax.rsqrt(jnp.mean(centred * centred, -1, keepdims=True) + norm_eps)
    return (centred * rstd, mean, rstd)


def norm_back(grad_n, normed, rstd):
    first = jnp.mean(grad_n, -1, keepdims=True)
    second = jnp.mean(grad_n * normed, -1, keepdims=True)
    return rstd * (grad_n - first - normed * second)


def gelu_both(v):
    c = math.sqrt(2.0 / math.pi)
    sq = v * v
    half = 0.5 + 0.5 * jnp.tanh(v * (c + c * 0.044715 * sq))
    act = v * half
    slope = half + act * (1.0 - half) * (2 * c + 6 * c * 0.044715 * sq)
    return act, slope


def full_spec(shape):
    return pl.BlockSpec(shape, lambda *_: (0,) * len(shape))


def mlp_kernel(
    own_rows, step_rows, h_ref, dm_ref, w1_ref, w2_ref, b1_ref,
    act_ref, dpre_ref, db_ref, own_ref, rest_ref, acc_ref,
):
    j = pl.program_id(0)

    @pl.when(j == 0)
    def _():
        acc_ref[...] = jnp.zeros_like(acc_ref)

    rows = h_ref.shape[0]
    w1, w2, b1 = w1_ref[...], w2_ref[...], b1_ref[...]
    total = jnp.zeros((1, w1.shape[1]), f32)
    for start in range(0, rows, step_rows):
        part = slice(start, start + step_rows)
        pre = dot_nn(h_ref[part, :], w1) + b1
        d_act = dot_nn(dm_ref[part, :], w2)
        act, slope = gelu_both(pre)
        d_pre = d_act * slope
        d_low = d_pre.astype(bf16)
        act_ref[part, :] = act.astype(bf16)
        dpre_ref[part, :] = d_low
        total = total + jnp.sum(d_pre, 0, keepdims=True)
        acc_ref[part, :] += dot_nt(d_low, w1)
    db_ref[...] = total

    @pl.when(j == pl.num_programs(0) - 1)
    def _():
        own_ref[...] = acc_ref[:own_rows, :]
        rest_ref[...] = acc_ref[own_rows:, :].astype(bf16)


def mlp_both(hidden_two, grad_m, mlp_w, bias, own_rows):
    rows, width = hidden_two.shape
    hidden = mlp_w.shape[1] // 2
    block = min(512, hidden)
    steps = hidden // block
    return pl.pallas_call(
        partial(mlp_kernel, own_rows, rows),
        grid=(steps,),
        in_specs=[
            full_spec((rows, width)),
            full_spec((rows, width)),
            pl.BlockSpec((width, block), lambda j: (0, j)),
            pl.BlockSpec((width, block), lambda j: (0, steps + j)),
            pl.BlockSpec((1, block), lambda j: (0, j)),
        ],
        out_specs=[
            pl.BlockSpec((rows, block), lambda j: (0, j)),
            pl.BlockSpec((rows, block), lambda j: (0, j)),
            pl.BlockSpec((1, block), lambda j: (0, j)),
            full_spec((own_rows, width)),
            full_spec((rows - own_rows, width)),
        ],
        out_shape=[
            jax.ShapeDtypeStruct((rows, hidden), bf16),
            jax.ShapeDtypeStruct((rows, hidden), bf16),
            jax.ShapeDtypeStruct((1, hidden), f32),
            jax.ShapeDtypeStruct((own_rows, width), f32),
            jax.ShapeDtypeStruct((rows - own_rows, width), bf16),
        ],
        scratch_shapes=[pltpu.VMEM((rows, width), f32)],
        compiler_params=pltpu.CompilerParams(vmem_limit_bytes=48 * MIB),
        cost_estimate=pl.CostEstimate(
            flops=6 * rows * width * hidden,
            bytes_accessed=4 * rows * hidden + 6 * width * hidden + 8 * rows * width,
            transcendentals=rows * hidden,
        ),
        name="mlp_both",
    )(hidden_two, grad_m, mlp_w, mlp_w, bias)


def transpose_low(value):
    return value.astype(f32).T.astype(bf16)


def mlp_grads_kernel(own_rows, half, h_ref, dm_ref, dpre_ref, act_ref, w2_ref, cot_ref, bias_ref, grad_ref, own_ref, rest_ref, sum_ref, h_t, dm_t, acc_ref):
    j = pl.program_id(0)

    @pl.when(j == 0)
    def _():
        h_t[...] = transpose_low(h_ref[...])
        dm_t[...] = transpose_low(dm_ref[...])
        acc_ref[...] = jnp.zeros_like(acc_ref)

    @pl.when(j < half)
    def _():
        grad_ref[...] = dot_nn(h_t[...], dpre_ref[...]).astype(bf16)

    @pl.when(j >= half)
    def _():
        grad_ref[...] = dot_nn(dm_t[...], act_ref[...]).astype(bf16)
        acc_ref[...] += dot_nt(act_ref[...], w2_ref[...])

    @pl.when(j == 2 * half - 1)
    def _():
        own_ref[...] = acc_ref[:own_rows, :]
        rest_ref[...] = acc_ref[own_rows:, :].astype(bf16)
        cot = cot_ref[...].astype(f32)
        total = jnp.sum(acc_ref[...] * cot, 0, keepdims=True)
        sum_ref[...] = total + bias_ref[...] * jnp.sum(cot[:own_rows], 0, keepdims=True)


def mlp_weight_grads(hidden_two, grad_m, grad_pre, activ, mlp_w, cot_all, bias, own_rows):
    rows, width = hidden_two.shape
    hidden = mlp_w.shape[1] // 2
    block = min(512, hidden)
    half = hidden // block
    return pl.pallas_call(
        partial(mlp_grads_kernel, own_rows, half),
        grid=(2 * half,),
        in_specs=[
            full_spec((rows, width)),
            full_spec((rows, width)),
            pl.BlockSpec((rows, block), lambda j: (0, jnp.minimum(j, half - 1))),
            pl.BlockSpec((rows, block), lambda j: (0, jnp.maximum(j - half, 0))),
            pl.BlockSpec((width, block), lambda j: (0, half + jnp.maximum(j - half, 0))),
            full_spec((rows, width)),
            full_spec((1, width)),
        ],
        out_specs=[
            pl.BlockSpec((width, block), lambda j: (0, j)),
            full_spec((own_rows, width)),
            full_spec((rows - own_rows, width)),
            full_spec((1, width)),
        ],
        out_shape=[
            jax.ShapeDtypeStruct((width, 2 * hidden), bf16),
            jax.ShapeDtypeStruct((own_rows, width), f32),
            jax.ShapeDtypeStruct((rows - own_rows, width), bf16),
            jax.ShapeDtypeStruct((1, width), f32),
        ],
        scratch_shapes=[
            pltpu.VMEM((width, rows), bf16),
            pltpu.VMEM((width, rows), bf16),
            pltpu.VMEM((rows, width), f32),
        ],
        compiler_params=pltpu.CompilerParams(vmem_limit_bytes=48 * MIB),
        cost_estimate=pl.CostEstimate(
            flops=6 * rows * width * hidden,
            bytes_accessed=4 * rows * hidden + 6 * width * hidden + 8 * rows * width,
            transcendentals=0,
        ),
        name="mlp_weight_grads",
    )(hidden_two, grad_m, grad_pre, activ, mlp_w, cot_all, bias)


def middle_kernel(own_steps, pieces, *refs):
    heads = [ref[...] for ref in refs[:pieces]]
    w_ref, x_ref, cot_ref, mod_ref = refs[pieces : pieces + 4]
    h_ref, dm_ref, sum_ref, a_ref, x1_ref, mean_ref, rstd_ref = refs[pieces + 4 :]
    i = pl.program_id(0)
    branch = dot_nt(jnp.concatenate(heads, 1), w_ref[...]) + mod_ref[6:7, :]
    middle = x_ref[...].astype(f32) + mod_ref[2:3, :] * branch
    normed, mean, rstd = normalize(middle)
    h_ref[...] = (normed * (1.0 + mod_ref[4:5, :]) + mod_ref[3:4, :]).astype(bf16)
    low = (mod_ref[5:6, :] * cot_ref[...].astype(f32)).astype(bf16)
    dm_ref[...] = low
    total = jnp.sum(low.astype(f32), 0, keepdims=True)

    @pl.when(i == 0)
    def _():
        sum_ref[...] = total

    @pl.when(i > 0)
    def _():
        sum_ref[...] += total

    @pl.when(i < own_steps)
    def _():
        a_ref[...] = branch
        x1_ref[...] = middle
        mean_ref[...] = mean
        rstd_ref[...] = rstd


def middle_part(heads, weight, x_all, cot_all, modul, own_rows):
    rows, width = x_all.shape
    block = min(256, own_rows)
    steps, own_steps = rows // block, own_rows // block
    specs, arrays = [], []
    for s, parts in enumerate(heads):
        for part in parts:
            specs.append(
                pl.BlockSpec(
                    (block, part.shape[1]),
                    partial(lambda back, i: (lax.rem(i - back + steps, steps), 0), s * own_steps),
                )
            )
            arrays.append(part)
    row_spec = pl.BlockSpec((block, width), lambda i: (i, 0))
    own_spec = pl.BlockSpec((block, width), lambda i: (jnp.minimum(i, own_steps - 1), 0))
    one_spec = pl.BlockSpec((block, 1), lambda i: (jnp.minimum(i, own_steps - 1), 0))
    return pl.pallas_call(
        partial(middle_kernel, own_steps, len(arrays)),
        grid=(steps,),
        in_specs=specs
        + [full_spec((width, width)), row_spec, row_spec, full_spec(modul.shape)],
        out_specs=[row_spec, row_spec, full_spec((1, width)), own_spec, own_spec, one_spec, one_spec],
        out_shape=[
            jax.ShapeDtypeStruct((rows, width), bf16),
            jax.ShapeDtypeStruct((rows, width), bf16),
            jax.ShapeDtypeStruct((1, width), f32),
            jax.ShapeDtypeStruct((own_rows, width), f32),
            jax.ShapeDtypeStruct((own_rows, width), f32),
            jax.ShapeDtypeStruct((own_rows, 1), f32),
            jax.ShapeDtypeStruct((own_rows, 1), f32),
        ],
        compiler_params=pltpu.CompilerParams(vmem_limit_bytes=40 * MIB),
        cost_estimate=pl.CostEstimate(
            flops=2 * rows * width * width,
            bytes_accessed=12 * rows * width + 8 * own_rows * width,
            transcendentals=rows,
        ),
        name="middle_part",
    )(*arrays, weight, x_all, cot_all, modul)


def middle_back_kernel(others, pieces, own_ref, *refs):
    arrived = refs[:others]
    cot_ref, x1_ref, a_ref, mean_ref, rstd_ref, mod_ref, w_ref = refs[others : others + 7]
    mid_ref, da_ref, sums_ref = refs[others + 7 : others + 10]
    head_refs = refs[others + 10 :]
    grad_h = own_ref[...]
    for ref in arrived:
        grad_h = grad_h + ref[...].astype(f32)
    normed = (x1_ref[...] - mean_ref[...]) * rstd_ref[...]
    grad_mid = cot_ref[...].astype(f32) + norm_back(
        grad_h * (1.0 + mod_ref[4:5, :]), normed, rstd_ref[...]
    )
    grad_a = (mod_ref[2:3, :] * grad_mid).astype(bf16)
    mid_ref[...] = grad_mid
    da_ref[...] = grad_a
    sums = jnp.concatenate(
        [
            jnp.sum(grad_mid * a_ref[...], 0, keepdims=True),
            jnp.sum(grad_h, 0, keepdims=True),
            jnp.sum(grad_h * normed, 0, keepdims=True),
            jnp.sum(grad_a.astype(f32), 0, keepdims=True),
        ]
    )
    i = pl.program_id(0)

    @pl.when(i == 0)
    def _():
        sums_ref[...] = sums

    @pl.when(i > 0)
    def _():
        sums_ref[...] += sums

    grad_heads = dot_nn(grad_a, w_ref[...]).astype(bf16)
    columns = head_refs[0].shape[1]
    for p in range(pieces):
        head_refs[p][...] = grad_heads[:, p * columns : (p + 1) * columns]


def middle_back(own, arrived, cot, x1, branch, mean, rstd, modul, weight, columns):
    rows, width = own.shape
    block = min(256, rows)
    pieces = width // columns
    row_spec = pl.BlockSpec((block, width), lambda i: (i, 0))
    one_spec = pl.BlockSpec((block, 1), lambda i: (i, 0))
    return pl.pallas_call(
        partial(middle_back_kernel, len(arrived), pieces),
        grid=(rows // block,),
        in_specs=[row_spec] * (len(arrived) + 4)
        + [one_spec, one_spec, full_spec(modul.shape), full_spec((width, width))],
        out_specs=[row_spec, row_spec, full_spec((4, width))]
        + [pl.BlockSpec((block, columns), lambda i: (i, 0))] * pieces,
        out_shape=[
            jax.ShapeDtypeStruct((rows, width), f32),
            jax.ShapeDtypeStruct((rows, width), bf16),
            jax.ShapeDtypeStruct((4, width), f32),
        ]
        + [jax.ShapeDtypeStruct((rows, columns), bf16)] * pieces,
        compiler_params=pltpu.CompilerParams(vmem_limit_bytes=40 * MIB),
        cost_estimate=pl.CostEstimate(
            flops=2 * rows * width * width, bytes_accessed=28 * rows * width, transcendentals=0
        ),
        name="middle_back",
    )(own, *arrived, cot, x1, branch, mean, rstd, modul, weight)


def col_grads_kernel(count, depth, arrays, core_ref, left_ref, *refs):
    keep_ref, send_ref = refs[arrays:]
    left_t = transpose_low(left_ref[...])
    core = core_ref[0]
    at = 0
    for ref in refs[:arrays]:
        for p in range(ref.shape[0]):
            columns = slice(at, at + ref.shape[2])
            result = dot_nn(left_t, ref[p])
            for i in range(count // 2):
                low = result[2 * i * depth : (2 * i + 1) * depth]
                high = result[(2 * i + 1) * depth : (2 * i + 2) * depth]
                rows = slice(i * depth, (i + 1) * depth)
                keep_ref[rows, columns] = jnp.where(core == 0, low, high).astype(bf16)
                send_ref[rows, columns] = jnp.where(core == 0, high, low).astype(bf16)
            at += ref.shape[2]


def col_grads(left, rights, core, depth):
    rows, width = left.shape
    columns = sum(right.shape[0] * right.shape[2] for right in rights)
    out = jax.ShapeDtypeStruct((width // 2, columns), bf16)
    vmem = pl.BlockSpec(memory_space=pltpu.VMEM)
    return pl.pallas_call(
        partial(col_grads_kernel, width // depth, depth, len(rights)),
        in_specs=[pl.BlockSpec(memory_space=pltpu.SMEM)] + [vmem] * (1 + len(rights)),
        out_specs=[vmem, vmem],
        out_shape=[out, out],
        compiler_params=pltpu.CompilerParams(vmem_limit_bytes=40 * MIB),
        cost_estimate=pl.CostEstimate(
            flops=2 * rows * width * columns,
            bytes_accessed=2 * rows * width + 4 * rows * columns,
            transcendentals=0,
        ),
        name="col_grads",
    )(core, left, *rights)


def hidden_back_kernel(own_steps, first, x_ref, w_ref, *refs):
    own_ref, rest_ref, sums_ref = refs[-3:]
    pieces = [ref[p] for ref in refs[:-3] for p in range(3)]
    total = dot_nt(jnp.concatenate(pieces, 1), w_ref[:, first:])
    normed, _, _ = normalize(x_ref[...].astype(f32))
    sums = jnp.concatenate(
        [jnp.sum(total, 0, keepdims=True), jnp.sum(total * normed, 0, keepdims=True)]
    )
    i = pl.program_id(0)

    @pl.when(i == 0)
    def _():
        sums_ref[...] = sums

    @pl.when(i > 0)
    def _():
        sums_ref[...] += sums

    @pl.when(i < own_steps)
    def _():
        own_ref[...] = total

    @pl.when(i >= own_steps)
    def _():
        rest_ref[...] = total.astype(bf16)


def hidden_back(x_all, grads, weight, first, own_rows):
    rows, width = x_all.shape
    columns = grads[0].shape[2]
    block = min(256, own_rows)
    own_steps = own_rows // block
    return pl.pallas_call(
        partial(hidden_back_kernel, own_steps, first),
        grid=(rows // block,),
        in_specs=[pl.BlockSpec((block, width), lambda i: (i, 0)), full_spec(weight.shape)]
        + [pl.BlockSpec((3, block, columns), lambda i: (0, i, 0))] * len(grads),
        out_specs=[
            pl.BlockSpec((block, width), lambda i: (jnp.minimum(i, own_steps - 1), 0)),
            pl.BlockSpec((block, width), lambda i: (jnp.maximum(i - own_steps, 0), 0)),
            full_spec((2, width)),
        ],
        out_shape=[
            jax.ShapeDtypeStruct((own_rows, width), f32),
            jax.ShapeDtypeStruct((rows - own_rows, width), bf16),
            jax.ShapeDtypeStruct((2, width), f32),
        ],
        compiler_params=pltpu.CompilerParams(vmem_limit_bytes=40 * MIB),
        cost_estimate=pl.CostEstimate(
            flops=6 * rows * width * columns * len(grads),
            bytes_accessed=4 * rows * width + 12 * rows * columns * len(grads),
            transcendentals=0,
        ),
        name="hidden_back",
    )(x_all, weight, *grads)


def shift(x, axis, step):
    size = lax.axis_size(axis)
    return lax.ppermute(x, axis, [(i, (i + step) % size) for i in range(size)])


def xor_step(x, axis, bit):
    size = lax.axis_size(axis)
    return lax.ppermute(x, axis, [(i, i ^ bit) for i in range(size)])


def bits_of(side_last):
    size = lax.axis_size("dp")
    bits = [1 << k for k in range(size.bit_length() - 1)]
    return bits[:1] + bits[2:] + bits[1:2] if side_last else bits


def xor_of(side_last):
    bits = bits_of(side_last)
    place = jnp.arange(1 << len(bits), dtype=jnp.int32)
    return sum(((place >> k) & 1) * bit for k, bit in enumerate(bits))


def xor_gather(x, side_last):
    return widen(x[None], bits_of(side_last))


def widen(out, bits):
    for bit in bits:
        out = jnp.concatenate([out, xor_step(out, "dp", bit)], 0)
    return out


def xor_scatter_sum(x, side_last):
    half = x.shape[0] // 2
    for bit in reversed(bits_of(side_last)):
        x = x[:half] + xor_step(x[half:], "dp", bit)
        half //= 2
    return x[0]


def xor_sum(x, side_last):
    for bit in bits_of(side_last):
        x = x + xor_step(x, "dp", bit)
    return x


def sort_xor(x, side_last):
    size = lax.axis_size("dp")
    me = lax.axis_index("dp")
    order = jnp.arange(size, dtype=jnp.int32)
    pick = ((order[:, None] ^ me) == xor_of(side_last)[None, :]).astype(f32)
    flat = x.reshape(size, -1).astype(f32)
    return jnp.dot(pick, flat, precision=highest).reshape(x.shape)


def rel_gather(x, axis):
    return [x] + [shift(x, axis, s) for s in range(1, lax.axis_size(axis))]


def sort_rel(parts, axis):
    size = lax.axis_size(axis)
    me = lax.axis_index(axis)
    out = []
    for target in range(size):
        value = jnp.zeros_like(parts[0])
        for s in range(size):
            value = jnp.where(lax.rem(me - s + size, size) == target, parts[s], value)
        out.append(value)
    return out


def together(run, work, *args):
    shapes = jax.eval_shape(work, *args)
    empty = lambda *_: jax.tree.map(lambda v: jnp.zeros(v.shape, v.dtype), shapes)
    return lax.cond(run, work, empty, *args)


def dp_place():
    size, me = lax.axis_size("dp"), lax.axis_index("dp")
    return size // 4, me // 4, lax.rem(me // 2, 2), lax.rem(me, 2)


def after(value, *others):
    return lax.optimization_barrier((value,) + others)[0]


def far_shift(x, step):
    size = lax.axis_size("dp")
    return lax.ppermute(x, "dp", [(i, (i + 4 * step) % size) for i in range(size)])


def add_low(keep, arrived):
    return (keep.astype(f32) + arrived.astype(f32)).astype(bf16)


def side_split(total, depth):
    far_size, _, side, _ = dp_place()
    total = total.reshape(far_size, 2, depth, total.shape[1])
    keep = lax.dynamic_index_in_dim(total, side, 1, keepdims=False)
    return keep, lax.dynamic_index_in_dim(total, 1 - side, 1, keepdims=False)


def far_split(total):
    far_size, far, _, _ = dp_place()
    rows = [
        lax.dynamic_index_in_dim(total, lax.rem(far + s, far_size), 0, keepdims=False)
        for s in range(far_size)
    ]
    return rows[0], rows[1:]


def shards(
    tokens, cond, cotangent, w_qkv, b_qv, w_proj, b_proj, w_fc1, b_fc1, w_fc2, b_fc2, w_ada, b_ada
):
    tensor_size = lax.axis_size("tensor")
    dp_size = lax.axis_size("dp")
    tensor_pos = lax.axis_index("tensor")
    dp_pos = lax.axis_index("dp")
    row_count, width = tokens.shape
    group_rows = row_count * tensor_size
    depth = w_qkv.shape[0]
    local_width = w_qkv.shape[2]
    hidden = w_fc1.shape[1]
    pairs = local_width // PAIR
    groups = 2 if pairs % 2 == 0 else 1
    group_width = local_width // groups
    assert cond.shape[0] == 1 and group_rows == LEN

    def row_sum(v):
        return jnp.sum(v, 0, dtype=f32)

    def cols_of(values, owner):
        return lax.dynamic_slice_in_dim(values, owner * local_width, local_width, values.ndim - 1)

    run = dp_pos >= 0
    qkv_parts = [
        w_qkv[:, :, g * group_width : (g + 1) * group_width].reshape(depth, 3 * group_width)
        for g in range(groups)
    ]
    attn_w = lax.all_gather(jnp.concatenate([w_proj.T] + qkv_parts, 1), "dp", axis=0, tiled=True)
    mlp_w = lax.all_gather(jnp.concatenate([w_fc1, w_fc2.T], 1), "dp", axis=0, tiled=True)
    x_all = jnp.concatenate(rel_gather(tokens, "tensor"), 0)
    core_one = lax.rem(dp_pos, 2).astype(jnp.int32).reshape(1)

    vectors = jnp.concatenate([b_qv.reshape(-1), b_fc1])
    packed = xor_gather(jnp.concatenate([cond.reshape(-1), vectors]), True)
    cond_all = packed[:, :width]
    own_vec = sort_xor(packed[:, width:], True)
    piece = b_proj.shape[0]
    n_fc1 = b_fc1.shape[0]
    qv_bias = own_vec[:, : 2 * piece].reshape(dp_size, 2, piece).transpose(1, 0, 2)
    qv_bias = qv_bias.reshape(2, local_width)
    fc1_bias = own_vec[:, 2 * piece :].reshape(1, hidden)

    silu_all = jax.nn.silu(cond_all.astype(f32)).astype(bf16)
    silu_own = lax.dynamic_slice(silu_all, (0, dp_pos * depth), (dp_size, depth))
    ada_flat = w_ada.reshape(depth, 6 * local_width)
    biases = jnp.concatenate([b_ada, b_proj[None], b_fc2[None]]).astype(f32)
    lane = lax.broadcasted_iota(jnp.int32, (1, local_width), 1)
    biases = jnp.where(lane // piece == dp_pos, jnp.tile(biases, (1, dp_size)), 0.0)
    mod_part = jnp.pad(dot_nn(silu_own, ada_flat), ((0, 0), (0, 2 * local_width)))
    mod_part = mod_part + biases.reshape(1, 8 * local_width)
    mod_half = xor_scatter_sum(mod_part, True).reshape(8, local_width)
    modul = jnp.concatenate(sort_rel(rel_gather(mod_half, "tensor"), "tensor"), 1)
    shift_one, scale_one, gate_one, shift_two, scale_two, gate_two, proj_bias, fc2_bias = [
        modul[k : k + 1] for k in range(8)
    ]

    def first_rows(cotangent, x_all, shift_one, scale_one):
        moved = rel_gather(cotangent, "tensor")[1:]
        normed, _, rstd = normalize(x_all.astype(f32))
        return moved, (normed * (1.0 + scale_one) + shift_one).astype(bf16)

    cot_parts, hidden_one = together(run, first_rows, cotangent, x_all, shift_one, scale_one)
    cot_all = jnp.concatenate([cotangent] + cot_parts, 0)
    normed_one, _, rstd_one = normalize(tokens.astype(f32))

    def attend_group(g, moving, hidden_one, attn_w, qv_bias):
        moved = rel_gather(moving, "tensor")[1:]
        cols = slice(g * group_width, (g + 1) * group_width)
        bias = jnp.concatenate([qv_bias[0, cols], jnp.zeros((group_width,), f32), qv_bias[1, cols]])
        at = local_width + 3 * group_width * g
        weight = attn_w[:, at : at + 3 * group_width]
        qkv = (dot_nn(hidden_one, weight) + bias).astype(bf16)
        return moved, qkv, attend(qkv, group_width)

    qkv, heads_out, lse, moved = [], [], [], []
    for g in range(groups):
        moving = heads_out[g - 1] if g else attn_w[:, :local_width]
        parts, qkv_g, (out, log_total) = together(
            run, partial(attend_group, g), moving, hidden_one, attn_w, qv_bias
        )
        qkv.append(qkv_g)
        heads_out.append(out)
        lse.append(log_total)
        moved.append(parts)
    moved.append(rel_gather(heads_out[-1], "tensor")[1:])
    proj_w = jnp.concatenate([attn_w[:, :local_width]] + moved[0], 1)
    heads_other = moved[1:]
    heads_rel = [heads_out] + [[v[s - 1] for v in heads_other] for s in range(1, tensor_size)]
    hidden_two, grad_m, dm_sum, branch_attn, middle, mean_two, rstd_two = middle_part(
        heads_rel, proj_w, x_all, cot_all, modul, row_count
    )

    activ, grad_pre, fc1_sum, own_two, rest_two = mlp_both(
        hidden_two, grad_m, mlp_w, fc1_bias, row_count
    )

    def owners_sum(own, rest):
        arrived = [
            shift(rest[(s - 1) * row_count : s * row_count], "tensor", -s)
            for s in range(1, tensor_size)
        ]
        return own, arrived

    def add_up(own, arrived):
        for part in arrived:
            own = own + part.astype(f32)
        return own

    def weight_part(rest_two, *args):
        arrived = owners_sum(None, rest_two)[1]
        return arrived, mlp_weight_grads(*args, row_count)

    arrived_two, (mlp_grads, own_mlp, rest_mlp, mlp_sum) = together(
        run, weight_part, rest_two, hidden_two, grad_m, grad_pre, activ, mlp_w, cot_all, fc2_bias
    )
    mlp_grads = lax.psum_scatter(mlp_grads, "dp", scatter_dimension=0, tiled=True)

    grad_mid, grad_a, sums_two, *grad_pieces = middle_back(
        own_two, arrived_two, cotangent, middle, branch_attn, mean_two, rstd_two, modul, proj_w, group_width
    )

    def heads_of(pieces, g):
        parts = [pieces[g]]
        for j in range(1, tensor_size):
            s = tensor_size - j
            parts.append(shift(pieces[s * groups + g], "tensor", -s))
        return jnp.concatenate(parts, 0)

    last = groups - 1
    grad_heads = heads_of(grad_pieces, 0)
    dqkv, early = [], []
    if last:

        def first_group(pieces, heads, qkv_g, lse_g, left):
            moved = heads_of(pieces, 1)
            grads = attend_back(qkv_g, heads, lse_g, group_width)
            return moved, grads, col_grads(left, [grads], core_one, depth)

        grad_heads, grads, early = together(
            run, first_group, grad_pieces, grad_heads, qkv[0], lse[0], hidden_one
        )
        dqkv.append(grads)

    def last_group(grad_a, early, heads, qkv_g, lse_g, before, x_all):
        grad_a_rows = jnp.concatenate(rel_gather(grad_a, "tensor"), 0)
        if early:
            early = add_low(early[0], xor_step(early[1], "dp", 1))
        grads = attend_back(qkv_g, heads, lse_g, group_width)
        back = hidden_back(x_all, before + [grads], attn_w, local_width, row_count)
        return grad_a_rows, early, grads, back

    grad_a_rows, early, grads, (own_one, rest_one, sums_one) = together(
        run, last_group, grad_a, early, grad_heads, qkv[last], lse[last], dqkv, x_all
    )
    dqkv = dqkv + [grads]

    grad_mod = jnp.concatenate([sums_one, sums_two[:3], mlp_sum, sums_two[3:]])
    grad_mod_own = cols_of(grad_mod, tensor_pos)
    for s in range(1, tensor_size):
        owner = lax.rem(tensor_pos - s + tensor_size, tensor_size)
        grad_mod_own = grad_mod_own + shift(cols_of(grad_mod, owner), "tensor", -s)
    grad_a_sum = grad_mod_own[6]
    grad_mod_own = grad_mod_own[:6].astype(bf16).reshape(6 * local_width)
    late = [
        jnp.concatenate(pair, 1)
        for pair in zip(
            col_grads(hidden_one, [dqkv[last]], core_one, depth),
            col_grads(grad_a_rows, [out[None] for out in heads_out], core_one, depth),
        )
    ]
    grad_vec = jnp.concatenate(
        [row_sum(d[0].astype(f32)) for d in dqkv]
        + [row_sum(d[2].astype(f32)) for d in dqkv]
        + [
            grad_a_sum,
            fc1_sum.reshape(-1),
            cols_of(dm_sum[0], tensor_pos),
        ]
    )

    late = add_low(late[0], xor_step(late[1], "dp", 1))
    total = jnp.concatenate([early, late], 1) if last else late
    side_keep, side_send = side_split(total, depth)

    def side_part(rest_one, side_keep, side_send, grad_mod_own, grad_vec):
        arrived = owners_sum(None, rest_one)[1]
        side = xor_step(side_send, "dp", 2)

        def small(grad_mod_own, grad_vec):
            grad_mod_all = xor_gather(grad_mod_own, True)
            silu_part = dot_nt(grad_mod_all, ada_flat)
            return grad_mod_all, silu_part, xor_sum(grad_vec, True)

        out = together(run, small, grad_mod_own, grad_vec)
        return arrived, far_split(add_low(side_keep, side)), out

    arrived_one, (far_own, far_sends), (grad_mod_all, silu_part, grad_vec) = together(
        run, side_part, rest_one, side_keep, side_send, grad_mod_own, grad_vec
    )

    def own_piece(values, start, size):
        return lax.dynamic_slice_in_dim(values, start + dp_pos * size, size, 0)

    def far_part(far_own, far_sends, rest_mlp, own_mlp, *args):
        arrived_mlp = owners_sum(None, rest_mlp)[1]
        far_arrived = [far_shift(part, s + 1) for s, part in enumerate(far_sends)]

        def small(silu_part, *values):
            near = widen(silu_part[None], bits_of(False)[:2])
            near, own_one, arrived_one, grad_mod_all, grad_vec, mlp_grads = lax.optimization_barrier(
                (near,) + values
            )
            silu_all = widen(near, bits_of(False)[2:])
            grad_hidden_one = add_up(own_one, arrived_one)
            grad_tokens = grad_mid + norm_back(
                grad_hidden_one * (1.0 + scale_one), normed_one, rstd_one
            )
            grad_ada = dot_tn(silu_own, grad_mod_all).reshape(depth, 6, local_width)
            ada_sum = jnp.sum(grad_mod_all, 0, dtype=f32).reshape(6, local_width)
            vectors = (
                lax.dynamic_slice_in_dim(ada_sum, dp_pos * piece, piece, 1),
                jnp.stack([own_piece(grad_vec, 0, piece), own_piece(grad_vec, local_width, piece)]),
                own_piece(grad_vec, 2 * local_width, piece),
                own_piece(grad_vec, 3 * local_width, n_fc1),
                own_piece(grad_vec, 3 * local_width + hidden, piece),
            )
            mlp_grads = mlp_grads.astype(f32)
            mlp_grads = (mlp_grads[:, :hidden], mlp_grads[:, hidden:].T)
            mine = (xor_of(False)[:, None] == xor_of(True)[None, :]).astype(f32)
            silu_rows = sort_xor(jnp.sum(silu_all * mine[:, :, None], 1), False)
            return grad_tokens.astype(bf16), silu_rows.reshape(1, width), grad_ada, vectors, mlp_grads

        out = together(run, small, *args)
        attn_grads = add_up(far_own.astype(f32), far_arrived)
        branch_mlp = add_up(own_mlp, arrived_mlp) + fc2_bias
        block_out = (middle + gate_two * branch_mlp).astype(bf16)
        return block_out, attn_grads, out

    block_out, attn_grads, out = together(
        run,
        far_part,
        far_own,
        far_sends,
        rest_mlp,
        own_mlp,
        silu_part,
        own_one,
        arrived_one,
        grad_mod_all,
        grad_vec,
        mlp_grads,
    )
    grad_tokens, silu_rows, grad_ada, vectors, (grad_fc1, grad_fc2) = out
    grad_ada_bias, grad_qv_bias, grad_proj_bias, grad_fc1_bias, grad_fc2_bias = vectors
    grad_silu = silu_rows
    for s in range(1, tensor_size):
        grad_silu = grad_silu + shift(silu_rows, "tensor", s)
    _, silu_back = jax.vjp(jax.nn.silu, cond.astype(f32))
    grad_cond = silu_back(grad_silu)[0]
    grad_qkv = attn_grads[:, : 3 * local_width].reshape(depth, groups, 3, group_width)
    grad_qkv = grad_qkv.transpose(0, 2, 1, 3).reshape(depth, 3, local_width)
    return (
        block_out,
        grad_tokens,
        grad_cond,
        grad_qkv,
        grad_qv_bias,
        attn_grads[:, 3 * local_width :].T,
        grad_proj_bias,
        grad_fc1,
        grad_fc1_bias,
        grad_fc2,
        grad_fc2_bias,
        grad_ada,
        grad_ada_bias,
    )


def solution(mesh):
    placed = (
        P(("dp", "tensor"), None),
        P("dp", None),
        P(("dp", "tensor"), None),
        P("dp", None, "tensor"),
        P(None, ("tensor", "dp")),
        P("tensor", "dp"),
        P(("tensor", "dp")),
        P("dp", "tensor"),
        P(("tensor", "dp")),
        P("tensor", "dp"),
        P(("tensor", "dp")),
        P("dp", None, "tensor"),
        P(None, ("tensor", "dp")),
    )
    return jax.shard_map(
        shards,
        mesh=mesh,
        in_specs=placed,
        out_specs=(
            P(("dp", "tensor"), None),
            P(("dp", "tensor"), None),
            P("dp", None),
            P("dp", None, "tensor"),
            P(None, ("tensor", "dp")),
            P("tensor", "dp"),
            P(("tensor", "dp")),
            P("dp", "tensor"),
            P(("tensor", "dp")),
            P("tensor", "dp"),
            P(("tensor", "dp")),
            P("dp", None, "tensor"),
            P(None, ("tensor", "dp")),
        ),
        check_vma=False,
    )
```
